256 devices in a mesh: dp: 8 (over z), expert: 32 (over y, x, core).
Axes of the slice: x: 4, y: 4, z: 8, core: 2. Of those that a mesh axis runs over, the one named last changes fastest.
Arguments:
- tokens: bfloat16 [16384, 2048], P(('dp', 'expert')), may hold values from -6 to 6
- row_cotangent: bfloat16 [16384, 8, 768], P(('dp', 'expert')), may hold values from -6 to 6
- routes: int32 [16384, 8], P(('dp', 'expert')), may hold values from 0 to 63, all different within a row; in each aligned block of 64 rows (0 to 63, 64 to 127, ...) at most 12 rows name the same one
- w_gate: bfloat16 [32, 2048, 768], P('expert'), may hold values from -0.125 to 0.125
- w_up: bfloat16 [32, 2048, 768], P('expert'), may hold values from -0.125 to 0.125
Outputs:
- grad_tokens: bfloat16 [16384, 2048], P(('dp', 'expert'))
- grad_gate: float32 [32, 2048, 768], P('expert', 'dp')
- grad_up: float32 [32, 2048, 768], P('expert', 'dp')
The draws below stay inside these ranges and needn't reach their ends.
Inputs may be any that keep to these rules, and one draw needn't show every extreme that they name: A token's 8 routes name distinct copies. Within the 64 tokens of one device no route is named by more than 12 tokens, a bound that some block reaches.
All inputs are finite; a program needn't handle non-finite values.
Results may differ from the reference program's by a relative error of at most 0.018.
Values may be sent and summed in bfloat16 or wider, within the bound.
A program may use at most 128 MiB of HBM per device.

```python
import math
import jax
import jax.numpy as jnp
import numpy as np
from jax import lax

D = 2048
FF = 768
K = 8
TOK_DEV = 64
E = 32
CAP = 12
TOKENS = 16384
N_DP = 8
N_EXPERT = 32


def level_of(stream_key, shape, pieces, low, largest):
    level = 1.0
    for position, blocks in pieces:
        steps = jax.random.uniform(jax.random.fold_in(jax.random.fold_in(stream_key, 6), position), (blocks,), jnp.float32, low / len(pieces), largest / len(pieces))
        level = level * jnp.repeat(jnp.exp(steps), shape[position] // blocks).reshape((-1,) + (1,) * (len(shape) - 1 - position))
    return level


def assign_block(own_key, own, number, rows, number_of, top, bound, lean):
    order = jax.random.permutation(own_key, number_of)
    crowded, ordinary = shares(number_of, rows * top, bound, lean, True), shares(number_of, rows * top, bound, lean, False)
    places = jnp.arange(number_of)

    def named(lengths, rotation):
        used = int((lengths > 0).sum())
        fixed = max(1, used // 4)
        passed = fixed + (places - fixed + rotation * (used - fixed)) % max(1, number_of - fixed)
        return jnp.zeros((number_of,), jnp.int32).at[order[jnp.where(places < fixed, places, passed)]].set(jnp.asarray(lengths, jnp.int32))

    lengths = jnp.where(number % 4 == 0, named(crowded, number // 4), named(ordinary, number - number // 4 - 1))
    mixed = jax.random.permutation(jax.random.fold_in(own, 3), number_of)
    giver, receiver = mixed[0:number_of // 2 * 2:2], mixed[1:number_of // 2 * 2:2]
    room = jnp.minimum(lengths[giver] - 1, bound - lengths[receiver]) // 2
    room = jnp.where((giver == order[0]) | (receiver == order[0]) | (lengths[receiver] == 0), 0, jnp.maximum(room, 0))
    passed = jax.random.randint(jax.random.fold_in(own, 4), (number_of // 2,), 0, 1 << 20) % (room + 1)
    lengths = lengths.at[giver].add(-passed).at[receiver].add(passed)
    items = jnp.searchsorted(jnp.cumsum(lengths), jnp.arange(rows * top), side="right").astype(jnp.int32)
    table = items.reshape(top, rows).T
    table = table[jax.random.permutation(jax.random.fold_in(own, 1), rows)]
    rotation = jax.random.randint(jax.random.fold_in(own, 2), (rows, 1), 0, top)
    return jnp.take_along_axis(table, (jnp.arange(top)[None, :] + rotation) % top, axis=1)


def shares(count, total, limit, slope, full):
    loads = [(1 << 20) // math.isqrt(standing ** slope) + 1 for standing in range(1, count + 1)]
    largest = limit if full else min(limit, max(-(-total // count), total * loads[0] // sum(loads)))
    least = 1 if total - largest >= count - 1 else 0
    holding, rest = [largest] + [least] * (count - 1), total - largest - least * (count - 1)
    while rest > 0:
        candidates = [i for i in range(1, count) if holding[i] < largest] or [i for i in range(1, count) if holding[i] < limit]
        pool, left = sum([loads[i] for i in candidates]), rest
        for i in candidates:
            addition = min(limit - holding[i], max(1, left * loads[i] // pool), rest)
            holding[i] = holding[i] + addition
            rest = rest - addition
    return np.array(holding)


def gaussian(own_key, dims, deviation, limit, split=(), kind=jnp.bfloat16):
    result = deviation * jax.random.normal(own_key, dims, jnp.float32)
    if split:
        result = result * level_of(own_key, dims, split, -0.22, 0.18)
    return jnp.clip(result, -limit, limit).astype(kind)


def setup_inputs(seed: int = 0) -> dict:
    key_of = jax.random.split(jax.random.key(seed), 6)
    tokens = gaussian(key_of[0], (TOKENS, D), 1.0, 6.0, ((0, 256),))
    row_cotangent = gaussian(key_of[1], (TOKENS, K, FF), 1.0, 6.0, ((0, 256),))
    routes_keys = jax.random.split(jax.random.fold_in(key_of[2], 1), TOKENS // TOK_DEV)
    routes_turns = jax.random.permutation(jax.random.fold_in(key_of[2], 3), TOKENS // TOK_DEV)
    routes = jax.vmap(lambda own, number: assign_block(jax.random.fold_in(key_of[2], 2), own, number, TOK_DEV, 2 * N_EXPERT, K, CAP, 1))(routes_keys, routes_turns).reshape((TOKENS, K))
    w_gate = gaussian(key_of[3], (E, D, FF), D ** -0.5, 0.125, ((0, 32),))
    w_up = gaussian(key_of[4], (E, D, FF), D ** -0.5, 0.125, ((0, 32),))
    return dict(tokens=tokens, row_cotangent=row_cotangent, routes=routes, w_gate=w_gate, w_up=w_up)


def slot_index(route_block, expert_count, capacity):
    flat_routes = route_block.reshape(-1).astype(jnp.int32)
    labels = jnp.arange(2 * expert_count, dtype=jnp.int32)
    one_hot = (flat_routes[:, None] == labels[None, :]).astype(jnp.int32)
    earlier = jnp.sum((jnp.cumsum(one_hot, axis=0) - 1) * one_hot, axis=1)
    host = flat_routes % expert_count
    kind = flat_routes // expert_count
    return ((host * 2 + kind) * capacity + earlier).astype(jnp.int32)


def expert_pass(rows_x, rows_dh, w_one, w_two):
    gate_proj = jnp.dot(rows_x, w_one, preferred_element_type=jnp.float32)
    up_proj = jnp.dot(rows_x, w_two, preferred_element_type=jnp.float32)
    sig_gate = jax.nn.sigmoid(gate_proj)
    cot_rows = rows_dh.astype(jnp.float32)
    d_gate = (cot_rows * up_proj * sig_gate * (1.0 + gate_proj * (1.0 - sig_gate))).astype(jnp.bfloat16)
    d_up = (cot_rows * gate_proj * sig_gate).astype(jnp.bfloat16)
    dims_back = (((1,), (1,)), ((), ()))
    back_rows = (lax.dot_general(d_gate, w_one, dims_back, preferred_element_type=jnp.float32)
                 + lax.dot_general(d_up, w_two, dims_back, preferred_element_type=jnp.float32)).astype(jnp.bfloat16)
    dims_weight = (((0,), (0,)), ((), ()))
    part_gate = lax.dot_general(rows_x, d_gate, dims_weight, preferred_element_type=jnp.float32).astype(jnp.bfloat16)
    part_up = lax.dot_general(rows_x, d_up, dims_weight, preferred_element_type=jnp.float32).astype(jnp.bfloat16)
    return back_rows, part_gate, part_up


def reference(tokens, row_cotangent, routes, w_gate, w_up):
    capacity = CAP
    half_axis = N_EXPERT // 2
    partner = jnp.bitwise_xor(jnp.arange(N_EXPERT, dtype=jnp.int32), half_axis)
    tok_blocks = tokens.reshape(N_DP, N_EXPERT, TOK_DEV, D)
    cot_blocks = row_cotangent.reshape(N_DP, N_EXPERT, TOK_DEV * K, FF)
    route_blocks = routes.reshape(N_DP, N_EXPERT, TOK_DEV, K)

    def build(x_block, c_block, pos):
        send_x = jnp.zeros((N_EXPERT * 2 * capacity, D), jnp.bfloat16).at[pos].set(jnp.repeat(x_block, K, axis=0))
        send_d = jnp.zeros((N_EXPERT * 2 * capacity, FF), jnp.bfloat16).at[pos].set(c_block)
        return send_x.reshape(N_EXPERT, 2 * capacity, D), send_d.reshape(N_EXPERT, 2 * capacity, FF)

    def one_group(carry, inputs):
        x_group, c_group, r_group = inputs
        positions = jax.vmap(lambda block: slot_index(block, N_EXPERT, capacity))(r_group)
        send_x, send_d = jax.vmap(build)(x_group, c_group, positions)
        recv_x = jnp.swapaxes(send_x, 0, 1)
        recv_d = jnp.swapaxes(send_d, 0, 1)

        def work(args):
            rx_all, rd_all, device = args
            other = jnp.bitwise_xor(device, half_axis)
            home_back, home_pg, home_pu = expert_pass(
                rx_all[:, :capacity].reshape(-1, D), rd_all[:, :capacity].reshape(-1, FF), w_gate[device], w_up[device])
            rep_back, rep_pg, rep_pu = expert_pass(
                rx_all[:, capacity:].reshape(-1, D), rd_all[:, capacity:].reshape(-1, FF), w_gate[other], w_up[other])
            back_all = jnp.concatenate([home_back.reshape(N_EXPERT, capacity, D),
                                        rep_back.reshape(N_EXPERT, capacity, D)], axis=1)
            return back_all, home_pg, home_pu, rep_pg, rep_pu

        backs, home_pg, home_pu, rep_pg, rep_pu = lax.map(
            work, (recv_x, recv_d, jnp.arange(N_EXPERT, dtype=jnp.int32)))
        grad_g = carry[0] + home_pg.astype(jnp.float32) + rep_pg[partner].astype(jnp.float32)
        grad_u = carry[1] + home_pu.astype(jnp.float32) + rep_pu[partner].astype(jnp.float32)
        returned = jnp.swapaxes(backs, 0, 1).reshape(N_EXPERT, N_EXPERT * 2 * capacity, D)

        def gather_back(ret_rows, pos):
            return ret_rows[pos].astype(jnp.float32).reshape(TOK_DEV, K, D).sum(axis=1).astype(jnp.bfloat16)

        token_grads = jax.vmap(gather_back)(returned, positions)
        return (grad_g, grad_u), token_grads

    start = (jnp.zeros((N_EXPERT, D, FF), jnp.float32), jnp.zeros((N_EXPERT, D, FF), jnp.float32))
    totals, token_grads = lax.scan(one_group, start, (tok_blocks, cot_blocks, route_blocks))
    return token_grads.reshape(TOKENS, D), totals[0] / N_DP, totals[1] / N_DP
```

```python
import jax
import jax.numpy as jnp
from jax import lax
from jax.sharding import PartitionSpec as P


def slot_index(route_block, expert_count, capacity):
    flat_routes = route_block.reshape(-1)
    labels = jnp.arange(2 * expert_count, dtype=jnp.int32)
    one_hot = (flat_routes[:, None] == labels[None, :]).astype(jnp.int32)
    earlier = jnp.sum((jnp.cumsum(one_hot, axis=0) - 1) * one_hot, axis=1)
    kind = flat_routes // expert_count
    home = jnp.bitwise_xor(flat_routes % expert_count, kind * (expert_count // 2))
    return (home * 2 + kind) * capacity + earlier


def expert_pass(rows_x, rows_dh, w_one, w_two):
    gate_proj = jnp.dot(rows_x, w_one, preferred_element_type=jnp.float32)
    up_proj = jnp.dot(rows_x, w_two, preferred_element_type=jnp.float32)
    sig_gate = jax.nn.sigmoid(gate_proj)
    cot_rows = rows_dh.astype(jnp.float32)
    d_gate = (cot_rows * up_proj * sig_gate * (1.0 + gate_proj * (1.0 - sig_gate))).astype(
        jnp.bfloat16
    )
    d_up = (cot_rows * gate_proj * sig_gate).astype(jnp.bfloat16)
    dims_back = (((1,), (1,)), ((), ()))
    back_rows = (
        lax.dot_general(d_gate, w_one, dims_back, preferred_element_type=jnp.float32)
        + lax.dot_general(d_up, w_two, dims_back, preferred_element_type=jnp.float32)
    ).astype(jnp.bfloat16)
    dims_weight = (((0,), (0,)), ((), ()))
    part_gate = lax.dot_general(
        rows_x, d_gate, dims_weight, preferred_element_type=jnp.float32
    ).astype(jnp.bfloat16)
    part_up = lax.dot_general(rows_x, d_up, dims_weight, preferred_element_type=jnp.float32).astype(
        jnp.bfloat16
    )
    return (back_rows, part_gate, part_up)


def body(tokens, row_cotangent, routes, w_gate, w_up):
    expert_count = lax.axis_size("expert")
    token_count = tokens.shape[0]
    top_k = routes.shape[1]
    model_width = tokens.shape[1]
    hidden = w_gate.shape[2]
    capacity = 3 * token_count * top_k // (4 * expert_count)
    position = slot_index(routes, expert_count, capacity)
    send_x = (
        jnp.zeros((expert_count * 2 * capacity, model_width), jnp.bfloat16)
        .at[position]
        .set(jnp.repeat(tokens, top_k, axis=0))
    )
    send_d = (
        jnp.zeros((expert_count * 2 * capacity, hidden), jnp.bfloat16)
        .at[position]
        .set(row_cotangent.reshape(-1, hidden))
    )
    recv_rows, recv_cots = (
        lax.all_to_all(
            send_x.reshape(expert_count, 2 * capacity, model_width),
            "expert",
            split_axis=0,
            concat_axis=0,
            tiled=True,
        ),
        lax.all_to_all(
            send_d.reshape(expert_count, 2 * capacity, hidden),
            "expert",
            split_axis=0,
            concat_axis=0,
            tiled=True,
        ),
    )
    back_all, gate_terms, up_terms = expert_pass(
        recv_rows.reshape(-1, model_width), recv_cots.reshape(-1, hidden), w_gate[0], w_up[0]
    )
    back_all = back_all.reshape(expert_count, 2 * capacity, model_width)
    gate_terms, up_terms = gate_terms[None], up_terms[None]
    returned = lax.all_to_all(back_all, "expert", split_axis=0, concat_axis=0, tiled=True).reshape(
        -1, model_width
    )
    grad_tokens = returned[position].astype(jnp.float32).reshape(token_count, top_k, model_width)
    grad_tokens = grad_tokens.sum(axis=1).astype(jnp.bfloat16)
    shard_gate, shard_up = (
        lax.psum_scatter(
            gate_terms, "dp", scatter_dimension=1, tiled=True
        ).astype(jnp.float32),
        lax.psum_scatter(
            up_terms, "dp", scatter_dimension=1, tiled=True
        ).astype(jnp.float32),
    )
    total_gate = shard_gate[0]
    total_up = shard_up[0]
    replicas = lax.axis_size("dp")
    return (grad_tokens, (total_gate / replicas)[None], (total_up / replicas)[None])


def solution(mesh):
    return jax.shard_map(
        body,
        mesh=mesh,
        in_specs=(
            P(("dp", "expert"), None),
            P(("dp", "expert"), None, None),
            P(("dp", "expert"), None),
            P("expert", None, None),
            P("expert", None, None),
        ),
        out_specs=(P(("dp", "expert"), None), P("expert", "dp", None), P("expert", "dp", None)),
        check_vma=False,
    )
```

```python
import functools

import jax
import jax.numpy as jnp
from jax import lax
from jax.experimental import pallas as pl
from jax.experimental.pallas import tpu as pltpu
from jax.sharding import PartitionSpec as P

MESH = pl.DeviceIdType.MESH
F32, BF16 = jnp.float32, jnp.bfloat16


def slot_index(route_block, expert_count, capacity):
    flat_routes = route_block.reshape(-1)
    labels = jnp.arange(2 * expert_count, dtype=jnp.int32)
    one_hot = (flat_routes[:, None] == labels[None, :]).astype(jnp.int32)
    earlier = jnp.sum((jnp.cumsum(one_hot, axis=0) - 1) * one_hot, axis=1)
    kind = flat_routes // expert_count
    home = jnp.bitwise_xor(flat_routes % expert_count, kind * (expert_count // 2))
    return (home * 2 + kind) * capacity + earlier


def expert_kernel(
    dims,
    xs_ref, dh_ref, pos_ref, wg_hbm, wu_hbm,
    gt_ref, gg_ref, gu_ref,
    w_ref, d_ref, ring_ref, part_ref, back_ref, ret_ref, comb_ref,
    w_sem, ring_send, ring_recv, ret_send, ret_recv, own_sem,
):
    n_dp, n_ex, slots, tok, top = dims
    width, hidden = w_ref.shape[1], w_ref.shape[2]
    rows = xs_ref.shape[0]
    cols = width // n_dp
    half = cols // 2
    me = lax.axis_index("expert")
    p = lax.axis_index("dp")
    w_copies = [
        pltpu.make_async_copy(src, w_ref.at[k], w_sem.at[k])
        for k, src in enumerate((wg_hbm, wu_hbm))
    ]
    for c in w_copies:
        c.start()
    barrier = pltpu.get_barrier_semaphore()
    right, left = lax.rem(p + 1, n_dp), lax.rem(p + n_dp - 1, n_dp)
    for z in (left, right):
        pl.semaphore_signal(barrier, inc=1, device_id={"dp": z}, device_id_type=MESH)

    def greet(k, c):
        pl.semaphore_signal(
            barrier, inc=1, device_id={"expert": lax.rem(me + k, n_ex)}, device_id_type=MESH
        )
        return c

    lax.fori_loop(1, n_ex, greet, 0)

    wide = 2 * n_ex * slots
    place = lax.broadcasted_iota(jnp.int32, (tok * top, wide), 1)
    row_of = lax.broadcasted_iota(jnp.int32, (tok, tok * top), 1)
    token_of = lax.broadcasted_iota(jnp.int32, (tok, tok * top), 0) * top
    group = jnp.where((row_of >= token_of) & (row_of < token_of + top), 1.0, 0.0).astype(BF16)
    for k in range(2):
        hit = jnp.where(place == pos_ref[...] + k * slots, 1.0, 0.0).astype(BF16)
        comb_ref[k * tok:(k + 1) * tok, :] = jnp.dot(
            group, hit, preferred_element_type=F32
        ).astype(BF16)

    for c in w_copies:
        c.wait()
    m_blk, n_blk = rows // 2, 256

    def gates(i, c):
        r = pl.ds(pl.multiple_of(i * m_blk, m_blk), m_blk)
        for n in range(hidden // n_blk):
            cs = slice(n * n_blk, (n + 1) * n_blk)
            g = jnp.dot(xs_ref[r, :], w_ref[0, :, cs], preferred_element_type=F32)
            u = jnp.dot(xs_ref[r, :], w_ref[1, :, cs], preferred_element_type=F32)
            s = jax.nn.sigmoid(g)
            h = dh_ref[r, cs].astype(F32)
            d_ref[r, cs] = (h * u * s * (1.0 + g * (1.0 - s))).astype(BF16)
            d_ref[r, hidden + n * n_blk:hidden + (n + 1) * n_blk] = (h * g * s).astype(BF16)
        return c

    lax.fori_loop(0, 2, gates, 0)

    def part(c, k):
        x_cols = xs_ref[:, pl.ds(pl.multiple_of(c * cols, cols), cols)]
        return lax.dot_general(
            x_cols, d_ref[:, k * hidden:(k + 1) * hidden],
            (((0,), (0,)), ((), ())), preferred_element_type=F32,
        )

    def chunk(s, k):
        return lax.rem(p + n_dp - 1 - s, n_dp) if k == 0 else lax.rem(p + 1 + s, n_dp)

    def ring_copy(s, k, b):
        sl = pl.ds(b * half, half)
        return pltpu.make_async_remote_copy(
            src_ref=ring_ref.at[k, s, sl],
            dst_ref=ring_ref.at[k, s + 1, sl],
            send_sem=ring_send.at[k, s, b],
            recv_sem=ring_recv.at[k, s, b],
            device_id={"dp": right if k == 0 else left},
            device_id_type=MESH,
        )

    pl.semaphore_wait(barrier, n_ex + 1)
    for k in range(2):
        ring_ref[k, 0] = part(chunk(0, k), k).astype(BF16)
        for b in range(2):
            ring_copy(0, k, b).start()

    side = 8
    wide_col = width // 2

    def back_chunk(i):
        y = lax.rem(me // side + i, n_ex // side)
        r = pl.ds(pl.multiple_of(y * side * slots, side * slots), side * slots)
        for h in range(2):
            wc = slice(h * wide_col, (h + 1) * wide_col)
            dims_back = (((1,), (1,)), ((), ()))
            b = lax.dot_general(
                d_ref[r, :hidden], w_ref[0, wc, :], dims_back, preferred_element_type=F32
            ) + lax.dot_general(
                d_ref[r, hidden:], w_ref[1, wc, :], dims_back, preferred_element_type=F32
            )
            part_rows = b.reshape(side, slots, wide_col)
            for j in range(side):
                back_ref[y * side + j, h * slots:(h + 1) * slots, :] = part_rows[j].astype(BF16)
        return y

    def ret_copy(t):
        return pltpu.make_async_remote_copy(
            src_ref=back_ref.at[t],
            dst_ref=ret_ref.at[me],
            send_sem=ret_send.at[t],
            recv_sem=ret_recv.at[me],
            device_id={"expert": t},
            device_id_type=MESH,
        )

    own_copy = pltpu.make_async_copy(back_ref.at[me], ret_ref.at[me], own_sem)

    def start_returns(i, y):
        def go(j, c):
            ret_copy(y * side + lax.rem(me + j, side)).start()
            return c

        if i == 0:
            own_copy.start()
            lax.fori_loop(1, side, go, 0)
        else:
            lax.fori_loop(0, side, go, 0)

    def ring_step(s):
        for k in range(2):
            part_ref[k] = part(chunk(s, k), k)
        for b in range(2):
            sl = pl.ds(b * half, half)
            for k in range(2):
                ring_copy(s - 1, k, b).wait_recv()
                ring_ref[k, s, sl] = (
                    ring_ref[k, s, sl].astype(F32) + part_ref[k, sl]
                ).astype(BF16)
                ring_copy(s, k, b).start()

    start_returns(0, back_chunk(0))
    ring_step(1)

    def both(s, c):
        start_returns(1, back_chunk(s - 1))
        ring_step(s)
        return c

    lax.fori_loop(2, 5, both, 0)

    def alone(s, c):
        ring_step(s)
        return c

    lax.fori_loop(5, n_dp - 1, alone, 0)
    scale = 1.0 / n_dp
    for k in range(2):
        part_ref[k] = part(p, k)
    for b in range(2):
        sl = pl.ds(b * half, half)
        for k, out in enumerate((gg_ref, gu_ref)):
            ring_copy(n_dp - 2, k, b).wait_recv()
            out[sl] = (ring_ref[k, n_dp - 1, sl].astype(F32) + part_ref[k, sl]) * scale

    def got(j, c):
        t = lax.rem(me + j, n_ex)
        pltpu.make_async_remote_copy(
            src_ref=back_ref.at[t], dst_ref=ret_ref.at[t], send_sem=ret_send.at[t],
            recv_sem=ret_recv.at[t], device_id={"expert": t}, device_id_type=MESH,
        ).wait()
        return c

    lax.fori_loop(1, n_ex, got, 0)
    own_copy.wait()
    summed = jnp.dot(
        comb_ref[...], ret_ref[...].reshape(wide, wide_col), preferred_element_type=F32
    )
    gt_ref[:, :wide_col] = summed[:tok].astype(BF16)
    gt_ref[:, wide_col:] = summed[tok:].astype(BF16)

    def sent(s, c):
        for k in range(2):
            for b in range(2):
                ring_copy(s, k, b).wait_send()
        return c

    lax.fori_loop(0, n_dp - 1, sent, 0)


def body(tokens, row_cotangent, routes, w_gate, w_up):
    n_ex, n_dp = lax.axis_size("expert"), lax.axis_size("dp")
    tok, width = tokens.shape
    top = routes.shape[1]
    hidden = w_gate.shape[2]
    capacity = 3 * tok * top // (4 * n_ex)
    slots = 2 * capacity
    rows = n_ex * slots
    position = slot_index(routes, n_ex, capacity)
    send_x = (
        jnp.zeros((rows, width), BF16).at[position].set(jnp.repeat(tokens, top, axis=0))
    )
    send_d = jnp.zeros((rows, hidden), BF16).at[position].set(row_cotangent.reshape(-1, hidden))
    recv_x, recv_d = (
        lax.all_to_all(
            a.reshape(n_ex, slots, -1), "expert", split_axis=0, concat_axis=0, tiled=True
        ).reshape(rows, -1)
        for a in (send_x, send_d)
    )
    pos_col = (position // slots * (2 * slots) + position % slots)[:, None]
    vmem = pl.BlockSpec(memory_space=pltpu.VMEM)
    hbm = pl.BlockSpec(memory_space=pl.ANY)
    cols = width // n_dp
    dma = pltpu.SemaphoreType.DMA
    gt, gg, gu = pl.pallas_call(
        functools.partial(expert_kernel, (n_dp, n_ex, slots, tok, top)),
        out_shape=(
            jax.ShapeDtypeStruct((tok, width), BF16),
            jax.ShapeDtypeStruct((cols, hidden), F32),
            jax.ShapeDtypeStruct((cols, hidden), F32),
        ),
        in_specs=[vmem, vmem, vmem, hbm, hbm],
        out_specs=(vmem, vmem, vmem),
        scratch_shapes=[
            pltpu.VMEM((2, width, hidden), BF16),
            pltpu.VMEM((rows, 2 * hidden), BF16),
            pltpu.VMEM((2, n_dp, cols, hidden), BF16),
            pltpu.VMEM((2, cols, hidden), F32),
            pltpu.VMEM((n_ex, 2 * slots, width // 2), BF16),
            pltpu.VMEM((n_ex, 2 * slots, width // 2), BF16),
            pltpu.VMEM((2 * tok, 2 * rows), BF16),
            dma((2,)),
            dma((2, n_dp, 2)),
            dma((2, n_dp, 2)),
            dma((n_ex,)),
            dma((n_ex,)),
            dma,
        ],
        compiler_params=pltpu.CompilerParams(
            collective_id=0, has_side_effects=True, vmem_limit_bytes=56 << 20
        ),
        name="expert_backward",
    )(recv_x, recv_d, pos_col, w_gate[0], w_up[0])
    return gt, gg[None], gu[None]


def solution(mesh):
    return jax.shard_map(
        body,
        mesh=mesh,
        in_specs=(
            P(("dp", "expert"), None),
            P(("dp", "expert"), None, None),
            P(("dp", "expert"), None),
            P("expert", None, None),
            P("expert", None, None),
        ),
        out_specs=(P(("dp", "expert"), None), P("expert", "dp", None), P("expert", "dp", None)),
        check_vma=False,
    )
```

```python
import functools

import jax
import jax.numpy as jnp
from jax import lax
from jax.experimental import pallas as pl
from jax.experimental.pallas import tpu as pltpu
from jax.sharding import PartitionSpec as P

MESH = pl.DeviceIdType.MESH
F32, BF16 = jnp.float32, jnp.bfloat16
SIDE = 4


def expert_kernel(
    dims,
    row_ref, col_ref, x_hbm, cot_hbm, wg_hbm, wu_hbm,
    gt_ref, gg_ref, gu_ref,
    w_ref, d_ref, ring_ref, part_ref, back_ref, ret_ref, comb_ref,
    cot_ref, xg_ref, xs_ref, dh_ref, dh_out, dh_in, all_ref, flat_ref, sel_ref,
    w_sem, ring_send, ring_recv, ret_send, ret_recv, own_sem,
    in_sem, ag_send, ag_recv, sib_send, sib_recv, dh_send, dh_recv, r_send, r_recv,
):
    n_dp, n_ex, slots, tok, top = dims
    width, hidden = w_ref.shape[1], w_ref.shape[2]
    rows = n_ex * slots
    cols = width // n_dp
    half = cols // 2
    me = lax.axis_index("expert")
    p = lax.axis_index("dp")
    core = lax.rem(me, 2)
    mx, my = lax.rem(me // 2, SIDE), me // (2 * SIDE)
    half_w = width // 2
    own_rows = pl.ds(pl.multiple_of(core * tok, tok), tok)
    loads = [
        pltpu.make_async_copy(
            x_hbm.at[:, pl.ds(h * half_w, half_w)], xg_ref.at[me // 2, h, own_rows], in_sem.at[h]
        )
        for h in range(2)
    ] + [pltpu.make_async_copy(cot_hbm, cot_ref, in_sem.at[2])]
    w_copies = [
        pltpu.make_async_copy(src, w_ref.at[k], w_sem.at[k])
        for k, src in enumerate((wg_hbm, wu_hbm))
    ]
    for c in loads + w_copies:
        c.start()
    barrier = pltpu.get_barrier_semaphore()
    right, left = lax.rem(p + 1, n_dp), lax.rem(p + n_dp - 1, n_dp)
    for z in (left, right):
        pl.semaphore_signal(barrier, inc=1, device_id={"dp": z}, device_id_type=MESH)

    def greet(k, c):
        pl.semaphore_signal(
            barrier, inc=1, device_id={"expert": lax.rem(me + k, n_ex)}, device_id_type=MESH
        )
        return c

    lax.fori_loop(1, n_ex, greet, 0)

    flat = tok * top
    early = lax.broadcasted_iota(jnp.int32, (flat, flat), 0)
    late = lax.broadcasted_iota(jnp.int32, (flat, flat), 1)
    same = col_ref[...] == row_ref[...]
    rank_row = jnp.sum(jnp.where(same & (early < late), 1.0, 0.0), axis=0, keepdims=True)
    rank_col = jnp.sum(jnp.where(same & (late < early), 1.0, 0.0), axis=1, keepdims=True)

    def placed(route, rank, stride):
        kind = jnp.where(route >= n_ex, 1, 0)
        home = route - kind * n_ex
        home = jnp.where(kind == 1, jnp.where(home >= n_ex // 2, home - n_ex // 2, home + n_ex // 2), home)
        return home * stride + kind * (slots // 2) + rank.astype(jnp.int32)

    pos_row = placed(row_ref[...], rank_row, slots)
    pos_col = placed(col_ref[...], rank_col, 2 * slots)

    wide = 2 * n_ex * slots
    place = lax.broadcasted_iota(jnp.int32, (flat, wide), 1)
    row_of = lax.broadcasted_iota(jnp.int32, (tok, flat), 1)
    token_of = lax.broadcasted_iota(jnp.int32, (tok, flat), 0) * top
    group = jnp.where((row_of >= token_of) & (row_of < token_of + top), 1.0, 0.0).astype(BF16)
    for k in range(2):
        hit = jnp.where(place == pos_col + k * slots, 1.0, 0.0).astype(BF16)
        comb_ref[k * tok:(k + 1) * tok, :] = jnp.dot(
            group, hit, preferred_element_type=F32
        ).astype(BF16)

    lot = 8
    loads[2].wait()

    def pack(i, c):
        spot = lax.broadcasted_iota(jnp.int32, (lot * slots, flat), 0) + i * (lot * slots)
        hit = jnp.where(spot == pos_row, 1.0, 0.0).astype(BF16)
        v = jnp.dot(hit, cot_ref[...], preferred_element_type=F32).reshape(lot, slots, hidden)
        for j in range(lot):
            for k in range(2):
                dh_out[i * lot + j, k * slots:(k + 1) * slots, :] = v[
                    j, :, k * (hidden // 2):(k + 1) * (hidden // 2)
                ].astype(BF16)
        return c

    lax.fori_loop(0, n_ex // lot, pack, 0)
    all_ref[me] = row_ref[...]
    for c in loads[:2]:
        c.wait()

    def chip_at(h, da, db):
        dx, dy = (da, db) if h == 0 else (db, da)
        return lax.rem(my + dy, SIDE) * SIDE + lax.rem(mx + dx, SIDE)

    def off(da, db):
        return (da % SIDE) * SIDE + db % SIDE

    def slab(h, da, db, lo, n, of_core):
        return xg_ref.at[
            chip_at(h, da % SIDE, db % SIDE), h,
            pl.ds(pl.multiple_of(of_core * tok + lo, tok // 2), n),
        ]

    sends = []

    def pass_on(h, da, db, axis, sign, piece=None):
        lo, n = (0, tok) if piece is None else (piece * (tok // 2), tok // 2)
        ra, rb = (da - sign, db) if axis == 0 else (da, db - sign)
        ta, tb = (sign % SIDE, 0) if axis == 0 else (0, sign % SIDE)
        ref = slab(h, da, db, lo, n, core)
        c = pltpu.make_async_remote_copy(
            src_ref=ref, dst_ref=ref,
            send_sem=ag_send.at[len(sends)],
            recv_sem=ag_recv.at[h, off(ra, rb), piece or 0],
            device_id={"expert": chip_at(h, ta, tb) * 2 + core},
            device_id_type=MESH,
        )
        c.start()
        sends.append(c)

    def arrived(h, da, db, piece=None):
        lo, n = (0, tok) if piece is None else (piece * (tok // 2), tok // 2)
        ref = slab(h, da, db, lo, n, core)
        pltpu.make_async_remote_copy(
            src_ref=ref, dst_ref=ref, send_sem=ag_send.at[0],
            recv_sem=ag_recv.at[h, off(da, db), piece or 0],
            device_id={"expert": me}, device_id_type=MESH,
        ).wait_recv()

    def sibling(h, da, db, of_core):
        ref = slab(h, da, db, 0, tok, of_core)
        return pltpu.make_async_remote_copy(
            src_ref=ref, dst_ref=ref,
            send_sem=sib_send.at[h, off(da, db)],
            recv_sem=sib_recv.at[h, off(da, db)],
            device_id={"expert": me + 1 - 2 * core},
            device_id_type=MESH,
        )

    def share(h, da, db):
        sibling(h, da, db, core).start()

    def select(h, da, db):
        sibling(h, da, db, 1 - core).wait_recv()
        chip = chip_at(h, da % SIDE, db % SIDE)
        xs_ref[
            pl.ds(pl.multiple_of(chip * 2 * slots, 2 * slots), 2 * slots),
            h * half_w:(h + 1) * half_w,
        ] = jnp.dot(sel_ref[chip], xg_ref[chip, h], preferred_element_type=F32).astype(BF16)

    def route_copy(t, slot):
        return pltpu.make_async_remote_copy(
            src_ref=all_ref.at[me], dst_ref=all_ref.at[slot],
            send_sem=r_send.at[t], recv_sem=r_recv.at[slot],
            device_id={"expert": t}, device_id_type=MESH,
        )

    def dh_copy(t, slot):
        return pltpu.make_async_remote_copy(
            src_ref=dh_out.at[t], dst_ref=dh_in.at[slot],
            send_sem=dh_send.at[t], recv_sem=dh_recv.at[slot],
            device_id={"expert": t}, device_id_type=MESH,
        )

    def peers(go):
        def one(k, c):
            go(lax.rem(me + k, n_ex))
            return c

        lax.fori_loop(1, n_ex, one, 0)

    pl.semaphore_wait(barrier, n_ex + 1)
    peers(lambda t: route_copy(t, me).start())
    for h in range(2):
        for sign in (1, -1):
            pass_on(h, 0, 0, 0, sign)
    for h in range(2):
        for sign in (1, -1):
            pass_on(h, 0, 0, 1, sign)
        share(h, 0, 0)

    peers(lambda t: route_copy(t, t).wait())
    for s in range(n_ex):
        flat_ref[s:s + 1, :] = all_ref[s].astype(F32)
    named = flat_ref[...]
    here = me.astype(F32)
    other = jnp.where(me >= n_ex // 2, me - n_ex // 2, me + n_ex // 2) + n_ex
    kinds = [jnp.where(named == v, 1.0, 0.0) for v in (here, other.astype(F32))]
    prior = jnp.where(early < late, 1.0, 0.0).astype(BF16)
    ranks = jnp.dot(
        jnp.concatenate(kinds, axis=0).astype(BF16), prior, preferred_element_type=F32
    )
    flat_ref[...] = (
        kinds[0] * (ranks[:n_ex] + 1.0) + kinds[1] * (ranks[n_ex:] + (1.0 + slots // 2)) - 1.0
    )
    token_lane = lax.broadcasted_iota(jnp.int32, (flat, 2 * tok), 1)
    token_lane = jnp.where(token_lane >= tok, token_lane - tok, token_lane) * top
    from_row = lax.broadcasted_iota(jnp.int32, (flat, 2 * tok), 0)
    to_token = jnp.where(
        (from_row >= token_lane) & (from_row < token_lane + top), 1.0, 0.0
    ).astype(BF16)
    spot_row = lax.broadcasted_iota(jnp.int32, (2 * slots, 2 * tok), 0) >= slots
    spot_lane = lax.broadcasted_iota(jnp.int32, (2 * slots, 2 * tok), 1) >= tok
    slot_no = lax.broadcasted_iota(jnp.int32, (slots, flat), 0).astype(F32)

    def choose(i, c):
        hits = [
            jnp.where(slot_no == flat_ref[pl.ds(2 * i + k, 1), :], 1.0, 0.0) for k in range(2)
        ]
        v = jnp.dot(
            jnp.concatenate(hits, axis=0).astype(BF16), to_token, preferred_element_type=F32
        )
        sel_ref[i] = jnp.where(spot_row == spot_lane, v, 0.0).astype(BF16)
        return c

    lax.fori_loop(0, n_ex // 2, choose, 0)

    both_ways = [(h, sign) for h in range(2) for sign in (1, -1)]
    for h, sign in both_ways:
        arrived(h, -sign, 0)
        pass_on(h, -sign, 0, 0, sign, 0 if sign == 1 else 1)
        pass_on(h, -sign, 0, 1, 1)
        pass_on(h, -sign, 0, 1, -1)
        share(h, -sign, 0)
    for h, sign in both_ways:
        arrived(h, 0, -sign)
        pass_on(h, 0, -sign, 1, sign, 0 if sign == 1 else 1)
        share(h, 0, -sign)
    for h in range(2):
        select(h, 0, 0)
    for h in range(2):
        for piece in range(2):
            arrived(h, 2, 0, piece)
        for sign in (1, -1):
            pass_on(h, 2, 0, 1, sign)
        share(h, 2, 0)
    for h in range(2):
        for da in (1, -1):
            select(h, da, 0)
    for da in (1, -1, 2):
        for h, sign in both_ways:
            arrived(h, da, -sign)
            pass_on(h, da, -sign, 1, sign, 0 if sign == 1 else 1)
            share(h, da, -sign)
    peers(lambda t: dh_copy(t, me).start())
    dh_own = pltpu.make_async_copy(dh_out.at[me], dh_in.at[me], in_sem.at[3])
    dh_own.start()
    for h in range(2):
        for da, db in ((0, 1), (0, -1), (2, 0), (1, 1), (1, -1), (-1, 1), (-1, -1)):
            select(h, da, db)
    for da in (0, 1, -1, 2):
        for h in range(2):
            for piece in range(2):
                arrived(h, da, 2, piece)
            share(h, da, 2)
    for h in range(2):
        for da, db in ((2, 1), (2, -1), (0, 2), (1, 2), (-1, 2), (2, 2)):
            select(h, da, db)
    peers(lambda t: dh_copy(t, t).wait())
    dh_own.wait()

    def unpack(i, c):
        v = dh_in[pl.ds(2 * i, 2)].astype(F32)
        r = pl.ds(pl.multiple_of(i * 2 * slots, 2 * slots), 2 * slots)
        for k in range(2):
            dh_ref[r, k * (hidden // 2):(k + 1) * (hidden // 2)] = (
                v[:, k * slots:(k + 1) * slots].reshape(2 * slots, hidden // 2).astype(BF16)
            )
        return c

    lax.fori_loop(0, n_ex // 2, unpack, 0)
    for c in w_copies:
        c.wait()
    m_blk, n_blk = rows // 2, 256

    def gates(i, c):
        r = pl.ds(pl.multiple_of(i * m_blk, m_blk), m_blk)
        for n in range(hidden // n_blk):
            cs = slice(n * n_blk, (n + 1) * n_blk)
            g = jnp.dot(xs_ref[r, :], w_ref[0, :, cs], preferred_element_type=F32)
            u = jnp.dot(xs_ref[r, :], w_ref[1, :, cs], preferred_element_type=F32)
            s = jax.nn.sigmoid(g)
            h = dh_ref[r, cs].astype(F32)
            d_ref[r, cs] = (h * u * s * (1.0 + g * (1.0 - s))).astype(BF16)
            d_ref[r, hidden + n * n_blk:hidden + (n + 1) * n_blk] = (h * g * s).astype(BF16)
        return c

    lax.fori_loop(0, 2, gates, 0)

    def part(c, k):
        x_cols = xs_ref[:, pl.ds(pl.multiple_of(c * cols, cols), cols)]
        return lax.dot_general(
            x_cols, d_ref[:, k * hidden:(k + 1) * hidden],
            (((0,), (0,)), ((), ())), preferred_element_type=F32,
        )

    def chunk(s, k):
        return lax.rem(p + n_dp - 1 - s, n_dp) if k == 0 else lax.rem(p + 1 + s, n_dp)

    def ring_copy(s, k, b):
        sl = pl.ds(b * half, half)
        return pltpu.make_async_remote_copy(
            src_ref=ring_ref.at[k, s, sl],
            dst_ref=ring_ref.at[k, s + 1, sl],
            send_sem=ring_send.at[k, s, b],
            recv_sem=ring_recv.at[k, s, b],
            device_id={"dp": right if k == 0 else left},
            device_id_type=MESH,
        )

    for k in range(2):
        ring_ref[k, 0] = part(chunk(0, k), k).astype(BF16)
        for b in range(2):
            ring_copy(0, k, b).start()

    side = 8
    wide_col = width // 2

    def back_chunk(i):
        y = lax.rem(me // side + i, n_ex // side)
        r = pl.ds(pl.multiple_of(y * side * slots, side * slots), side * slots)
        for h in range(2):
            wc = slice(h * wide_col, (h + 1) * wide_col)
            dims_back = (((1,), (1,)), ((), ()))
            b = lax.dot_general(
                d_ref[r, :hidden], w_ref[0, wc, :], dims_back, preferred_element_type=F32
            ) + lax.dot_general(
                d_ref[r, hidden:], w_ref[1, wc, :], dims_back, preferred_element_type=F32
            )
            part_rows = b.reshape(side, slots, wide_col)
            for j in range(side):
                back_ref[y * side + j, h * slots:(h + 1) * slots, :] = part_rows[j].astype(BF16)
        return y

    def ret_copy(t):
        return pltpu.make_async_remote_copy(
            src_ref=back_ref.at[t],
            dst_ref=ret_ref.at[me],
            send_sem=ret_send.at[t],
            recv_sem=ret_recv.at[me],
            device_id={"expert": t},
            device_id_type=MESH,
        )

    own_copy = pltpu.make_async_copy(back_ref.at[me], ret_ref.at[me], own_sem)

    def start_returns(i, y):
        def go(j, c):
            ret_copy(y * side + lax.rem(me + j, side)).start()
            return c

        if i == 0:
            own_copy.start()
            lax.fori_loop(1, side, go, 0)
        else:
            lax.fori_loop(0, side, go, 0)

    def ring_step(s):
        for k in range(2):
            part_ref[k] = part(chunk(s, k), k)
        for b in range(2):
            sl = pl.ds(b * half, half)
            for k in range(2):
                ring_copy(s - 1, k, b).wait_recv()
                ring_ref[k, s, sl] = (
                    ring_ref[k, s, sl].astype(F32) + part_ref[k, sl]
                ).astype(BF16)
                ring_copy(s, k, b).start()

    start_returns(0, back_chunk(0))
    ring_step(1)

    def both(s, c):
        start_returns(1, back_chunk(s - 1))
        ring_step(s)
        return c

    lax.fori_loop(2, 5, both, 0)

    def alone(s, c):
        ring_step(s)
        return c

    lax.fori_loop(5, n_dp - 1, alone, 0)
    scale = 1.0 / n_dp
    for k in range(2):
        part_ref[k] = part(p, k)
    for b in range(2):
        sl = pl.ds(b * half, half)
        for k, out in enumerate((gg_ref, gu_ref)):
            ring_copy(n_dp - 2, k, b).wait_recv()
            out[sl] = (ring_ref[k, n_dp - 1, sl].astype(F32) + part_ref[k, sl]) * scale

    def got(j, c):
        t = lax.rem(me + j, n_ex)
        pltpu.make_async_remote_copy(
            src_ref=back_ref.at[t], dst_ref=ret_ref.at[t], send_sem=ret_send.at[t],
            recv_sem=ret_recv.at[t], device_id={"expert": t}, device_id_type=MESH,
        ).wait()
        return c

    lax.fori_loop(1, n_ex, got, 0)
    own_copy.wait()
    summed = jnp.dot(
        comb_ref[...], ret_ref[...].reshape(wide, wide_col), preferred_element_type=F32
    )
    gt_ref[:, :wide_col] = summed[:tok].astype(BF16)
    gt_ref[:, wide_col:] = summed[tok:].astype(BF16)

    def sent(s, c):
        for k in range(2):
            for b in range(2):
                ring_copy(s, k, b).wait_send()
        return c

    lax.fori_loop(0, n_dp - 1, sent, 0)
    for c in sends:
        c.wait_send()
    for h in range(2):
        for da in range(SIDE):
            for db in range(SIDE):
                sibling(h, da, db, core).wait_send()


def body(tokens, row_cotangent, routes, w_gate, w_up):
    n_ex, n_dp = lax.axis_size("expert"), lax.axis_size("dp")
    tok, width = tokens.shape
    top = routes.shape[1]
    hidden = w_gate.shape[2]
    capacity = 3 * tok * top // (4 * n_ex)
    slots = 2 * capacity
    rows = n_ex * slots
    flat = tok * top
    vmem = pl.BlockSpec(memory_space=pltpu.VMEM)
    hbm = pl.BlockSpec(memory_space=pl.ANY)
    cols = width // n_dp
    dma = pltpu.SemaphoreType.DMA
    gt, gg, gu = pl.pallas_call(
        functools.partial(expert_kernel, (n_dp, n_ex, slots, tok, top)),
        out_shape=(
            jax.ShapeDtypeStruct((tok, width), BF16),
            jax.ShapeDtypeStruct((cols, hidden), F32),
            jax.ShapeDtypeStruct((cols, hidden), F32),
        ),
        in_specs=[vmem, vmem, hbm, hbm, hbm, hbm],
        out_specs=(vmem, vmem, vmem),
        scratch_shapes=[
            pltpu.VMEM((2, width, hidden), BF16),
            pltpu.VMEM((rows, 2 * hidden), BF16),
            pltpu.VMEM((2, n_dp, cols, hidden), BF16),
            pltpu.VMEM((2, cols, hidden), F32),
            pltpu.VMEM((n_ex, 2 * slots, width // 2), BF16),
            pltpu.VMEM((n_ex, 2 * slots, width // 2), BF16),
            pltpu.VMEM((2 * tok, 2 * rows), BF16),
            pltpu.VMEM((flat, hidden), BF16),
            pltpu.VMEM((n_ex // 2, 2, 2 * tok, width // 2), BF16),
            pltpu.VMEM((rows, width), BF16),
            pltpu.VMEM((rows, hidden), BF16),
            pltpu.VMEM((n_ex, 2 * slots, hidden // 2), BF16),
            pltpu.VMEM((n_ex, 2 * slots, hidden // 2), BF16),
            pltpu.VMEM((n_ex, 1, flat), jnp.int32),
            pltpu.VMEM((n_ex, flat), F32),
            pltpu.VMEM((n_ex // 2, 2 * slots, 2 * tok), BF16),
            dma((2,)),
            dma((2, n_dp, 2)),
            dma((2, n_dp, 2)),
            dma((n_ex,)),
            dma((n_ex,)),
            dma,
            dma((4,)),
            dma((40,)),
            dma((2, SIDE * SIDE, 2)),
            dma((2, SIDE * SIDE)),
            dma((2, SIDE * SIDE)),
            dma((n_ex,)),
            dma((n_ex,)),
            dma((n_ex,)),
            dma((n_ex,)),
        ],
        compiler_params=pltpu.CompilerParams(
            collective_id=0, has_side_effects=True, vmem_limit_bytes=56 << 20
        ),
        name="expert_backward",
    )(
        routes.reshape(1, flat), routes.reshape(flat, 1), tokens,
        row_cotangent.reshape(flat, hidden), w_gate[0], w_up[0],
    )
    return gt, gg[None], gu[None]


def solution(mesh):
    return jax.shard_map(
        body,
        mesh=mesh,
        in_specs=(
            P(("dp", "expert"), None),
            P(("dp", "expert"), None, None),
            P(("dp", "expert"), None),
            P("expert", None, None),
            P("expert", None, None),
        ),
        out_specs=(P(("dp", "expert"), None), P("expert", "dp", None), P("expert", "dp", None)),
        check_vma=False,
    )
```

```python
import functools

import jax
import jax.numpy as jnp
from jax import lax
from jax.experimental import pallas as pl
from jax.experimental.pallas import tpu as pltpu
from jax.sharding import PartitionSpec as P

MESH = pl.DeviceIdType.MESH
F32, BF16 = jnp.float32, jnp.bfloat16
SIDE = 4
ROUND = (
    (1, 0), (3, 0), (0, 1), (0, 3), (1, 1), (3, 3), (1, 3), (3, 1),
    (2, 0), (0, 2), (2, 1), (1, 2), (2, 3), (3, 2), (2, 2),
)


def expert_kernel(
    dims,
    routes_ref, x_hbm, cot_hbm, wg_hbm, wu_hbm,
    gt_ref, gg_ref, gu_ref,
    w_ref, d_ref, ring_ref, part_ref, back_ref, ret_ref, comb_ref,
    cot_ref, xg_ref, xs_ref, gate_ref, dh_out, dh_in, all_ref, flat_ref, sel_ref,
    w_sem, ring_send, ring_recv, ret_send, ret_recv, own_sem,
    in_sem, ag_send, ag_recv, sib_send, sib_recv, dh_send, dh_recv, r_send, r_recv,
):
    n_dp, n_ex, slots, tok, top = dims
    width, hidden = w_ref.shape[1], w_ref.shape[2]
    rows = n_ex * slots
    cols = width // n_dp
    third = hidden // 3
    lane = third // 2
    me = lax.axis_index("expert")
    p = lax.axis_index("dp")
    core = lax.rem(me, 2)
    mx, my = lax.rem(me // 2, SIDE), me // (2 * SIDE)
    half_w = width // 2
    own_rows = pl.ds(pl.multiple_of(core * tok, tok), tok)
    loads = [
        pltpu.make_async_copy(
            x_hbm.at[:, pl.ds(h * half_w, half_w)], xg_ref.at[me // 2, h, own_rows], in_sem.at[h]
        )
        for h in range(2)
    ] + [pltpu.make_async_copy(cot_hbm, cot_ref, in_sem.at[2])]
    w_copies = [
        pltpu.make_async_copy(src, w_ref.at[k], w_sem.at[k])
        for k, src in enumerate((wg_hbm, wu_hbm))
    ]
    for c in loads + w_copies:
        c.start()
    barrier = pltpu.get_barrier_semaphore()
    right, left = lax.rem(p + 1, n_dp), lax.rem(p + n_dp - 1, n_dp)
    for z in (left, right):
        pl.semaphore_signal(barrier, inc=1, device_id={"dp": z}, device_id_type=MESH)

    def greet(k, c):
        pl.semaphore_signal(
            barrier, inc=1, device_id={"expert": lax.rem(me + k, n_ex)}, device_id_type=MESH
        )
        return c

    lax.fori_loop(1, n_ex, greet, 0)

    flat = tok * top
    early = lax.broadcasted_iota(jnp.int32, (flat, flat), 0)
    late = lax.broadcasted_iota(jnp.int32, (flat, flat), 1)
    row_of = lax.broadcasted_iota(jnp.int32, (tok, flat), 1)
    token_of = lax.broadcasted_iota(jnp.int32, (tok, flat), 0) * top
    group = jnp.where((row_of >= token_of) & (row_of < token_of + top), 1.0, 0.0).astype(BF16)
    named = routes_ref[...].astype(F32).astype(BF16)
    over_first = (((0,), (0,)), ((), ()))
    by_row = jnp.dot(named, group, preferred_element_type=F32)
    by_col = lax.dot_general(group, named, (((0,), (1,)), ((), ())), preferred_element_type=F32)
    j_row = lax.broadcasted_iota(jnp.int32, (top, flat), 0)
    j_col = lax.broadcasted_iota(jnp.int32, (flat, top), 1)
    at_row = lax.rem(lax.broadcasted_iota(jnp.int32, (top, flat), 1), top)
    at_col = lax.rem(lax.broadcasted_iota(jnp.int32, (flat, top), 0), top)
    route_row = jnp.sum(jnp.where(j_row == at_row, by_row, 0.0), axis=0, keepdims=True)
    route_col = jnp.sum(jnp.where(j_col == at_col, by_col, 0.0), axis=1, keepdims=True)
    same = route_col == route_row
    rank_row = jnp.sum(jnp.where(same & (early < late), 1.0, 0.0), axis=0, keepdims=True)
    rank_col = jnp.sum(jnp.where(same & (late < early), 1.0, 0.0), axis=1, keepdims=True)

    def placed(route, rank, stride):
        kind = jnp.where(route >= n_ex, 1.0, 0.0)
        home = route - kind * n_ex
        away = jnp.where(home >= n_ex // 2, home - n_ex // 2, home + n_ex // 2)
        home = jnp.where(kind > 0.5, away, home)
        return (home * stride + kind * (slots // 2) + rank).astype(jnp.int32)

    pos_row = placed(route_row, rank_row, slots)
    pos_col = placed(route_col, rank_col, 2 * slots)

    wide = 2 * n_ex * slots
    place = lax.broadcasted_iota(jnp.int32, (flat, wide), 1)
    for k in range(2):
        hit = jnp.where(place == pos_col + k * slots, 1.0, 0.0).astype(BF16)
        comb_ref[k * tok:(k + 1) * tok, :] = jnp.dot(
            group, hit, preferred_element_type=F32
        ).astype(BF16)

    lot = 8
    loads[2].wait()

    def pack(i, c):
        spot = lax.broadcasted_iota(jnp.int32, (lot * slots, flat), 0) + i * (lot * slots)
        hit = jnp.where(spot == pos_row, 1.0, 0.0).astype(BF16)
        v = jnp.dot(hit, cot_ref[...], preferred_element_type=F32).reshape(lot, slots, hidden)
        for j in range(lot):
            for k in range(6):
                dh_out[i * lot + j, k * slots:(k + 1) * slots, :] = v[
                    j, :, k * lane:(k + 1) * lane
                ].astype(BF16)
        return c

    lax.fori_loop(0, n_ex // lot, pack, 0)
    all_ref[me] = route_row
    for c in loads[:2]:
        c.wait()

    def chip_at(h, da, db):
        dx, dy = (da, db) if h == 0 else (db, da)
        return lax.rem(my + dy, SIDE) * SIDE + lax.rem(mx + dx, SIDE)

    def off(da, db):
        return (da % SIDE) * SIDE + db % SIDE

    def slab(h, da, db, lo, n, of_core):
        return xg_ref.at[
            chip_at(h, da % SIDE, db % SIDE), h,
            pl.ds(pl.multiple_of(of_core * tok + lo, tok // 2), n),
        ]

    sends = []

    def pass_on(h, da, db, axis, sign, piece=None):
        lo, n = (0, tok) if piece is None else (piece * (tok // 2), tok // 2)
        ra, rb = (da - sign, db) if axis == 0 else (da, db - sign)
        ta, tb = (sign % SIDE, 0) if axis == 0 else (0, sign % SIDE)
        ref = slab(h, da, db, lo, n, core)
        c = pltpu.make_async_remote_copy(
            src_ref=ref, dst_ref=ref,
            send_sem=ag_send.at[len(sends)],
            recv_sem=ag_recv.at[h, off(ra, rb), piece or 0],
            device_id={"expert": chip_at(h, ta, tb) * 2 + core},
            device_id_type=MESH,
        )
        c.start()
        sends.append(c)

    def arrived(h, da, db, piece=None):
        lo, n = (0, tok) if piece is None else (piece * (tok // 2), tok // 2)
        ref = slab(h, da, db, lo, n, core)
        pltpu.make_async_remote_copy(
            src_ref=ref, dst_ref=ref, send_sem=ag_send.at[0],
            recv_sem=ag_recv.at[h, off(da, db), piece or 0],
            device_id={"expert": me}, device_id_type=MESH,
        ).wait_recv()

    def sibling(h, da, db, of_core):
        ref = slab(h, da, db, 0, tok, of_core)
        return pltpu.make_async_remote_copy(
            src_ref=ref, dst_ref=ref,
            send_sem=sib_send.at[h, off(da, db)],
            recv_sem=sib_recv.at[h, off(da, db)],
            device_id={"expert": me + 1 - 2 * core},
            device_id_type=MESH,
        )

    def share(h, da, db):
        sibling(h, da, db, core).start()

    def select(h, da, db):
        sibling(h, da, db, 1 - core).wait_recv()
        chip = chip_at(h, da % SIDE, db % SIDE)
        xs_ref[
            pl.ds(pl.multiple_of(chip * 2 * slots, 2 * slots), 2 * slots),
            h * half_w:(h + 1) * half_w,
        ] = jnp.dot(sel_ref[chip], xg_ref[chip, h], preferred_element_type=F32).astype(BF16)

    def route_copy(t, slot):
        return pltpu.make_async_remote_copy(
            src_ref=all_ref.at[me], dst_ref=all_ref.at[slot],
            send_sem=r_send.at[t], recv_sem=r_recv.at[slot],
            device_id={"expert": t}, device_id_type=MESH,
        )

    def dh_piece(ref, q):
        return ref.at[pl.ds(q * 2 * slots, 2 * (q + 1) * slots)]

    def dh_copy(t, slot, q):
        return pltpu.make_async_remote_copy(
            src_ref=dh_piece(dh_out.at[t], q), dst_ref=dh_piece(dh_in.at[slot], q),
            send_sem=dh_send.at[q, t], recv_sem=dh_recv.at[q, slot],
            device_id={"expert": t}, device_id_type=MESH,
        )

    def peers(go):
        def one(k, c):
            go(lax.rem(me + k, n_ex))
            return c

        lax.fori_loop(1, n_ex, one, 0)

    def to_peers(go):
        for dx, dy in ROUND:
            for dc in range(2):
                go(chip_at(0, dx, dy) * 2 + lax.rem(core + dc, 2))
        go(me + 1 - 2 * core)

    pl.semaphore_wait(barrier, n_ex + 1)
    for h in range(2):
        for sign in (1, -1):
            pass_on(h, 0, 0, 0, sign)
    peers(lambda t: route_copy(t, me).start())
    for h in range(2):
        for sign in (1, -1):
            pass_on(h, 0, 0, 1, sign)
        share(h, 0, 0)
    to_peers(lambda t: dh_copy(t, me, 0).start())

    both_ways = [(h, sign) for h in range(2) for sign in (1, -1)]
    for h, sign in both_ways:
        arrived(h, -sign, 0)
        pass_on(h, -sign, 0, 0, sign, 0 if sign == 1 else 1)
    for h, sign in both_ways:
        pass_on(h, -sign, 0, 1, 1)
        pass_on(h, -sign, 0, 1, -1)
        share(h, -sign, 0)
    for h, sign in both_ways:
        arrived(h, 0, -sign)
        pass_on(h, 0, -sign, 1, sign, 0 if sign == 1 else 1)
        share(h, 0, -sign)
    for h in range(2):
        for piece in range(2):
            arrived(h, 2, 0, piece)
        for sign in (1, -1):
            pass_on(h, 2, 0, 1, sign)
        share(h, 2, 0)

    peers(lambda t: route_copy(t, t).wait())
    for s in range(n_ex):
        flat_ref[s:s + 1, :] = all_ref[s]
    named = flat_ref[...]
    here = me.astype(F32)
    other = jnp.where(me >= n_ex // 2, me - n_ex // 2, me + n_ex // 2) + n_ex
    kinds = [jnp.where(named == v, 1.0, 0.0) for v in (here, other.astype(F32))]
    prior = jnp.where(early < late, 1.0, 0.0).astype(BF16)
    ranks = jnp.dot(
        jnp.concatenate(kinds, axis=0).astype(BF16), prior, preferred_element_type=F32
    )
    flat_ref[...] = (
        kinds[0] * (ranks[:n_ex] + 1.0) + kinds[1] * (ranks[n_ex:] + (1.0 + slots // 2)) - 1.0
    )
    token_lane = lax.broadcasted_iota(jnp.int32, (flat, 2 * tok), 1)
    token_lane = jnp.where(token_lane >= tok, token_lane - tok, token_lane) * top
    from_row = lax.broadcasted_iota(jnp.int32, (flat, 2 * tok), 0)
    to_token = jnp.where(
        (from_row >= token_lane) & (from_row < token_lane + top), 1.0, 0.0
    ).astype(BF16)
    spot_row = lax.broadcasted_iota(jnp.int32, (2 * slots, 2 * tok), 0) >= slots
    spot_lane = lax.broadcasted_iota(jnp.int32, (2 * slots, 2 * tok), 1) >= tok
    slot_no = lax.broadcasted_iota(jnp.int32, (slots, flat), 0).astype(F32)

    def choose(i, c):
        hits = [
            jnp.where(slot_no == flat_ref[pl.ds(2 * i + k, 1), :], 1.0, 0.0) for k in range(2)
        ]
        v = jnp.dot(
            jnp.concatenate(hits, axis=0).astype(BF16), to_token, preferred_element_type=F32
        )
        sel_ref[i] = jnp.where(spot_row == spot_lane, v, 0.0).astype(BF16)
        return c

    lax.fori_loop(0, n_ex // 2, choose, 0)

    for h in range(2):
        select(h, 0, 0)
    for h in range(2):
        for da in (1, -1):
            select(h, da, 0)
    for da in (1, -1, 2):
        for h, sign in both_ways:
            arrived(h, da, -sign)
            pass_on(h, da, -sign, 1, sign, 0 if sign == 1 else 1)
            share(h, da, -sign)
    dh_own = pltpu.make_async_copy(dh_out.at[me], dh_in.at[me], in_sem.at[3])
    dh_own.start()
    for h in range(2):
        for da, db in ((0, 1), (0, -1), (2, 0), (1, 1), (1, -1), (-1, 1), (-1, -1)):
            select(h, da, db)
    for da in (0, 1, -1, 2):
        for h in range(2):
            for piece in range(2):
                arrived(h, da, 2, piece)
            share(h, da, 2)
    to_peers(lambda t: dh_copy(t, me, 1).start())
    for h in range(2):
        for da, db in ((2, 1), (2, -1), (0, 2), (1, 2), (-1, 2), (2, 2)):
            select(h, da, db)
    for c in w_copies:
        c.wait()
    m_blk = rows // 2

    def gates(b):
        def one(i, c):
            r = pl.ds(pl.multiple_of(i * m_blk, m_blk), m_blk)
            for k in range(2):
                gate_ref[k, r] = jnp.dot(
                    xs_ref[r, :], w_ref[k, :, b * third:(b + 1) * third],
                    preferred_element_type=F32,
                )
            return c

        lax.fori_loop(0, 2, one, 0)

    def cotangents(b):
        def one(i, c):
            n = 2 * slots
            r = pl.ds(pl.multiple_of(i * n, n), n)
            v = dh_in[pl.ds(2 * i, 2), b * n:(b + 1) * n].astype(F32)
            for k in range(2):
                cs = slice(k * lane, (k + 1) * lane)
                h = v[:, k * slots:(k + 1) * slots].reshape(n, lane)
                g, u = gate_ref[0, r, cs], gate_ref[1, r, cs]
                s = jax.nn.sigmoid(g)
                at = b * third + k * lane
                d_ref[r, at:at + lane] = (h * u * s * (1.0 + g * (1.0 - s))).astype(BF16)
                d_ref[r, hidden + at:hidden + at + lane] = (h * g * s).astype(BF16)
            return c

        lax.fori_loop(0, n_ex // 2, one, 0)

    def part(c, k, b):
        x_cols = xs_ref[:, pl.ds(pl.multiple_of(c * cols, cols), cols)]
        at = k * hidden + b * third
        return lax.dot_general(
            x_cols, d_ref[:, at:at + third], over_first, preferred_element_type=F32
        )

    def chunk(s, k):
        return lax.rem(p + 2 * n_dp - 1 - s, n_dp) if k == 0 else lax.rem(p + 1 + s, n_dp)

    def ring_copy(s, k, b):
        return pltpu.make_async_remote_copy(
            src_ref=ring_ref.at[k, s, b],
            dst_ref=ring_ref.at[k, s + 1, b],
            send_sem=ring_send.at[k, s, b],
            recv_sem=ring_recv.at[k, s, b],
            device_id={"dp": right if k == 0 else left},
            device_id_type=MESH,
        )

    def begin(b):
        gates(b)
        if b == 0:
            peers(lambda t: dh_copy(t, t, 0).wait())
            dh_own.wait()
        if b == 1:
            peers(lambda t: dh_copy(t, t, 1).wait())
        cotangents(b)
        for k in range(2):
            ring_ref[k, 0, b] = part(chunk(0, k), k, b).astype(BF16)
            ring_copy(0, k, b).start()
        for k in range(2):
            part_ref[k, b] = part(chunk(1, k), k, b)

    def unit(s, b):
        for k in range(2):
            ring_copy(s - 1, k, b).wait_recv()
            ring_ref[k, s, b] = (ring_ref[k, s, b].astype(F32) + part_ref[k, b]).astype(BF16)
            ring_copy(s, k, b).start()
        for k in range(2):
            part_ref[k, b] = part(chunk(s + 1, k), k, b)

    begin(0)
    begin(1)
    unit(1, 0)
    begin(2)
    side = 8
    wide_col = width // 2

    def back_half(i, h):
        y = lax.rem(me // side + i, n_ex // side)
        r = pl.ds(pl.multiple_of(y * side * slots, side * slots), side * slots)
        wc = slice(h * wide_col, (h + 1) * wide_col)
        dims_back = (((1,), (1,)), ((), ()))
        b = lax.dot_general(
            d_ref[r, :hidden], w_ref[0, wc, :], dims_back, preferred_element_type=F32
        ) + lax.dot_general(
            d_ref[r, hidden:], w_ref[1, wc, :], dims_back, preferred_element_type=F32
        )
        part_rows = b.reshape(side, slots, wide_col)
        for j in range(side):
            back_ref[y * side + j, h * slots:(h + 1) * slots, :] = part_rows[j].astype(BF16)
        return y

    def ret_copy(t):
        return pltpu.make_async_remote_copy(
            src_ref=back_ref.at[t],
            dst_ref=ret_ref.at[me],
            send_sem=ret_send.at[t],
            recv_sem=ret_recv.at[me],
            device_id={"expert": t},
            device_id_type=MESH,
        )

    own_copy = pltpu.make_async_copy(back_ref.at[me], ret_ref.at[me], own_sem)

    def start_returns(i, y):
        if i == 0:
            own_copy.start()
        for dx in (1, 3, 0, 2):
            for dc in range(2):
                if (i, dx, dc) != (0, 0, 0):
                    ret_copy(y * side + lax.rem(mx + dx, SIDE) * 2 + lax.rem(core + dc, 2)).start()

    back_half(0, 0)
    unit(1, 1)
    start_returns(0, back_half(0, 1))
    unit(1, 2)
    back_half(1, 0)
    unit(2, 0)
    start_returns(1, back_half(1, 1))
    unit(2, 1)
    back_half(3, 0)
    unit(2, 2)
    start_returns(3, back_half(3, 1))
    unit(3, 0)
    back_half(2, 0)
    unit(3, 1)
    start_returns(2, back_half(2, 1))
    unit(3, 2)

    def alone(s, c):
        for b in range(3):
            unit(s, b)
        return c

    lax.fori_loop(4, n_dp - 1, alone, 0)
    def got(j, c):
        t = lax.rem(me + j, n_ex)
        pltpu.make_async_remote_copy(
            src_ref=back_ref.at[t], dst_ref=ret_ref.at[t], send_sem=ret_send.at[t],
            recv_sem=ret_recv.at[t], device_id={"expert": t}, device_id_type=MESH,
        ).wait()
        return c

    lax.fori_loop(1, n_ex, got, 0)
    own_copy.wait()
    summed = jnp.dot(
        comb_ref[...], ret_ref[...].reshape(wide, wide_col), preferred_element_type=F32
    )
    gt_ref[:, :wide_col] = summed[:tok].astype(BF16)
    gt_ref[:, wide_col:] = summed[tok:].astype(BF16)

    scale = 1.0 / n_dp
    for b in range(3):
        for k, out in enumerate((gg_ref, gu_ref)):
            ring_copy(n_dp - 2, k, b).wait_recv()
            out[:, b * third:(b + 1) * third] = (
                ring_ref[k, n_dp - 1, b].astype(F32) + part_ref[k, b]
            ) * scale

    def sent(s, c):
        for k in range(2):
            for b in range(3):
                ring_copy(s, k, b).wait_send()
        return c

    lax.fori_loop(0, n_dp - 1, sent, 0)
    for c in sends:
        c.wait_send()
    for h in range(2):
        for da in range(SIDE):
            for db in range(SIDE):
                sibling(h, da, db, core).wait_send()


def hand_over(a, b, c, x, y, z, u, v, w, sem):
    loads = [
        pltpu.make_async_copy(src, held, sem.at[0, k])
        for k, (src, held) in enumerate(((a, u), (b, v), (c, w)))
    ]
    stores = [
        pltpu.make_async_copy(held, dst, sem.at[1, k])
        for k, (held, dst) in enumerate(((u, x), (v, y), (w, z)))
    ]
    for copy in loads:
        copy.start()
    for load, store in zip(loads, stores):
        load.wait()
        store.start()
    for copy in stores:
        copy.wait()


def body(tokens, row_cotangent, routes, w_gate, w_up):
    n_ex, n_dp = lax.axis_size("expert"), lax.axis_size("dp")
    tok, width = tokens.shape
    top = routes.shape[1]
    hidden = w_gate.shape[2]
    capacity = 3 * tok * top // (4 * n_ex)
    slots = 2 * capacity
    rows = n_ex * slots
    flat = tok * top
    vmem = pl.BlockSpec(memory_space=pltpu.VMEM)
    hbm = pl.BlockSpec(memory_space=pl.ANY)
    cols = width // n_dp
    dma = pltpu.SemaphoreType.DMA
    grads = pl.pallas_call(
        functools.partial(expert_kernel, (n_dp, n_ex, slots, tok, top)),
        out_shape=(
            jax.ShapeDtypeStruct((tok, width), BF16),
            jax.ShapeDtypeStruct((cols, hidden), F32),
            jax.ShapeDtypeStruct((cols, hidden), F32),
        ),
        in_specs=[vmem, hbm, hbm, hbm, hbm],
        out_specs=(vmem, vmem, vmem),
        scratch_shapes=[
            pltpu.VMEM((2, width, hidden), BF16),
            pltpu.VMEM((rows, 2 * hidden), BF16),
            pltpu.VMEM((2, n_dp, 3, cols, hidden // 3), BF16),
            pltpu.VMEM((2, 3, cols, hidden // 3), F32),
            pltpu.VMEM((n_ex, 2 * slots, width // 2), BF16),
            pltpu.VMEM((n_ex, 2 * slots, width // 2), BF16),
            pltpu.VMEM((2 * tok, 2 * rows), BF16),
            pltpu.VMEM((flat, hidden), BF16),
            pltpu.VMEM((n_ex // 2, 2, 2 * tok, width // 2), BF16),
            pltpu.VMEM((rows, width), BF16),
            pltpu.VMEM((2, rows, hidden // 3), F32),
            pltpu.VMEM((n_ex, 6 * slots, hidden // 6), BF16),
            pltpu.VMEM((n_ex, 6 * slots, hidden // 6), BF16),
            pltpu.VMEM((n_ex, 1, flat), F32),
            pltpu.VMEM((n_ex, flat), F32),
            pltpu.VMEM((n_ex // 2, 2 * slots, 2 * tok), BF16),
            dma((2,)),
            dma((2, n_dp, 3)),
            dma((2, n_dp, 3)),
            dma((n_ex,)),
            dma((n_ex,)),
            dma,
            dma((4,)),
            dma((40,)),
            dma((2, SIDE * SIDE, 2)),
            dma((2, SIDE * SIDE)),
            dma((2, SIDE * SIDE)),
            dma((2, n_ex)),
            dma((2, n_ex)),
            dma((n_ex,)),
            dma((n_ex,)),
        ],
        compiler_params=pltpu.CompilerParams(
            collective_id=0, has_side_effects=True, vmem_limit_bytes=56 << 20
        ),
        name="expert_backward",
    )(
        routes.T, tokens, row_cotangent.reshape(flat, hidden), w_gate[0], w_up[0],
    )
    gt, gg, gu = pl.pallas_call(
        hand_over,
        out_shape=tuple(jax.ShapeDtypeStruct(g.shape, g.dtype) for g in grads),
        in_specs=[hbm] * 3,
        out_specs=[hbm] * 3,
        scratch_shapes=[pltpu.VMEM(g.shape, g.dtype) for g in grads] + [dma((2, 3))],
        name="hand_over",
    )(*grads)
    return gt, gg[None], gu[None]


def solution(mesh):
    return jax.shard_map(
        body,
        mesh=mesh,
        in_specs=(
            P(("dp", "expert"), None),
            P(("dp", "expert"), None, None),
            P(("dp", "expert"), None),
            P("expert", None, None),
            P("expert", None, None),
        ),
        out_specs=(P(("dp", "expert"), None), P("expert", "dp", None), P("expert", "dp", None)),
        check_vma=False,
    )
```

```python
import functools

import jax
import jax.numpy as jnp
from jax import lax
from jax.experimental import pallas as pl
from jax.experimental.pallas import tpu as pltpu
from jax.sharding import PartitionSpec as P

MESH = pl.DeviceIdType.MESH
F32, BF16 = jnp.float32, jnp.bfloat16
SIDE = 4
ROUND = (
    (1, 0), (3, 0), (0, 1), (0, 3), (1, 1), (3, 3), (1, 3), (3, 1),
    (2, 0), (0, 2), (2, 1), (1, 2), (2, 3), (3, 2), (2, 2),
)


def expert_kernel(
    dims,
    routes_ref, x_hbm, cot_hbm, wg_hbm, wu_hbm,
    gt_ref, gg_ref, gu_ref,
    w_ref, d_ref, ring_ref, part_ref, back_ref, ret_ref, comb_ref,
    cot_ref, xg_ref, xs_ref, gate_ref, dh_out, dh_in, all_ref, flat_ref, sel_ref,
    mine_ref, gt_buf, g_buf,
    w_sem, ring_send, ring_recv, ret_send, ret_recv, out_sem,
    in_sem, ag_send, ag_recv, sib_send, sib_recv, dh_send, dh_recv, r_send, r_recv,
):
    n_dp, n_ex, slots, tok, top = dims
    width, hidden = w_ref.shape[1], w_ref.shape[2]
    rows = n_ex * slots
    cols = width // n_dp
    third = hidden // 3
    lane = third // 2
    me = lax.axis_index("expert")
    p = lax.axis_index("dp")
    core = lax.rem(me, 2)
    mx, my = lax.rem(me // 2, SIDE), me // (2 * SIDE)
    half_w = width // 2
    own_rows = pl.ds(pl.multiple_of(core * tok, tok), tok)
    loads = [
        pltpu.make_async_copy(
            x_hbm.at[:, pl.ds(h * half_w, half_w)], xg_ref.at[me // 2, h, own_rows], in_sem.at[h]
        )
        for h in range(2)
    ] + [pltpu.make_async_copy(cot_hbm, cot_ref, in_sem.at[2])]
    w_copies = [
        pltpu.make_async_copy(src, w_ref.at[k], w_sem.at[k])
        for k, src in enumerate((wg_hbm, wu_hbm))
    ]
    for c in loads + w_copies:
        c.start()
    barrier = pltpu.get_barrier_semaphore()
    right, left = lax.rem(p + 1, n_dp), lax.rem(p + n_dp - 1, n_dp)
    for z in (left, right):
        pl.semaphore_signal(barrier, inc=1, device_id={"dp": z}, device_id_type=MESH)

    def greet(k, c):
        pl.semaphore_signal(
            barrier, inc=1, device_id={"expert": lax.rem(me + k, n_ex)}, device_id_type=MESH
        )
        return c

    lax.fori_loop(1, n_ex, greet, 0)

    for c in loads[:2]:
        c.wait()

    def chip_at(h, da, db):
        dx, dy = (da, db) if h == 0 else (db, da)
        return lax.rem(my + dy, SIDE) * SIDE + lax.rem(mx + dx, SIDE)

    def off(da, db):
        return (da % SIDE) * SIDE + db % SIDE

    def slab(h, da, db, lo, n, of_core):
        return xg_ref.at[
            chip_at(h, da % SIDE, db % SIDE), h,
            pl.ds(pl.multiple_of(of_core * tok + lo, tok // 2), n),
        ]

    sends = []

    def pass_on(h, da, db, axis, sign, piece=None):
        lo, n = (0, tok) if piece is None else (piece * (tok // 2), tok // 2)
        ra, rb = (da - sign, db) if axis == 0 else (da, db - sign)
        ta, tb = (sign % SIDE, 0) if axis == 0 else (0, sign % SIDE)
        ref = slab(h, da, db, lo, n, core)
        c = pltpu.make_async_remote_copy(
            src_ref=ref, dst_ref=ref,
            send_sem=ag_send.at[len(sends)],
            recv_sem=ag_recv.at[h, off(ra, rb), piece or 0],
            device_id={"expert": chip_at(h, ta, tb) * 2 + core},
            device_id_type=MESH,
        )
        c.start()
        sends.append(c)

    def arrived(h, da, db, piece=None):
        lo, n = (0, tok) if piece is None else (piece * (tok // 2), tok // 2)
        ref = slab(h, da, db, lo, n, core)
        pltpu.make_async_remote_copy(
            src_ref=ref, dst_ref=ref, send_sem=ag_send.at[0],
            recv_sem=ag_recv.at[h, off(da, db), piece or 0],
            device_id={"expert": me}, device_id_type=MESH,
        ).wait_recv()

    def sibling(h, da, db, of_core):
        ref = slab(h, da, db, 0, tok, of_core)
        return pltpu.make_async_remote_copy(
            src_ref=ref, dst_ref=ref,
            send_sem=sib_send.at[h, off(da, db)],
            recv_sem=sib_recv.at[h, off(da, db)],
            device_id={"expert": me + 1 - 2 * core},
            device_id_type=MESH,
        )

    def share(h, da, db):
        sibling(h, da, db, core).start()

    def select(h, da, db):
        sibling(h, da, db, 1 - core).wait_recv()
        chip = chip_at(h, da % SIDE, db % SIDE)
        xs_ref[
            pl.ds(pl.multiple_of(chip * 2 * slots, 2 * slots), 2 * slots),
            h * half_w:(h + 1) * half_w,
        ] = jnp.dot(sel_ref[chip], xg_ref[chip, h], preferred_element_type=F32).astype(BF16)

    def route_copy(t, slot):
        return pltpu.make_async_remote_copy(
            src_ref=mine_ref, dst_ref=all_ref.at[slot],
            send_sem=r_send, recv_sem=r_recv,
            device_id={"expert": t}, device_id_type=MESH,
        )

    def dh_piece(ref, q):
        lanes = pl.ds(q * 2 * slots, 2 * (q + 1) * slots)
        return ref.at[:, lanes] if len(ref.shape) == 3 else ref.at[lanes]

    def dh_copy(t, slot, q):
        return pltpu.make_async_remote_copy(
            src_ref=dh_piece(dh_out.at[t], q), dst_ref=dh_piece(dh_in.at[slot], q),
            send_sem=dh_send.at[q], recv_sem=dh_recv.at[q],
            device_id={"expert": t}, device_id_type=MESH,
        )

    def landed(ref, sem):
        pltpu.make_async_copy(ref, ref, sem).wait()

    def keep_own(own, to, sem):
        pltpu.make_async_copy(own, to, sem).start()

    def peers(go):
        def one(k, c):
            go(lax.rem(me + k, n_ex))
            return c

        lax.fori_loop(1, n_ex, one, 0)

    def to_peers(go):
        for dx, dy in ROUND:
            for dc in range(2):
                go(chip_at(0, dx, dy) * 2 + lax.rem(core + dc, 2))
        go(me + 1 - 2 * core)

    pl.semaphore_wait(barrier, n_ex + 1)
    for h in range(2):
        for sign in (1, -1):
            pass_on(h, 0, 0, 0, sign)
    for h in range(2):
        for sign in (1, -1):
            pass_on(h, 0, 0, 1, sign)
        share(h, 0, 0)
    flat = tok * top
    early = lax.broadcasted_iota(jnp.int32, (flat, flat), 0)
    late = lax.broadcasted_iota(jnp.int32, (flat, flat), 1)
    row_of = lax.broadcasted_iota(jnp.int32, (tok, flat), 1)
    token_of = lax.broadcasted_iota(jnp.int32, (tok, flat), 0) * top
    group = jnp.where((row_of >= token_of) & (row_of < token_of + top), 1.0, 0.0).astype(BF16)
    named = routes_ref[...].astype(F32).astype(BF16)
    over_first = (((0,), (0,)), ((), ()))
    by_row = jnp.dot(named, group, preferred_element_type=F32)
    by_col = lax.dot_general(group, named, (((0,), (1,)), ((), ())), preferred_element_type=F32)
    j_row = lax.broadcasted_iota(jnp.int32, (top, flat), 0)
    j_col = lax.broadcasted_iota(jnp.int32, (flat, top), 1)
    at_row = lax.rem(lax.broadcasted_iota(jnp.int32, (top, flat), 1), top)
    at_col = lax.rem(lax.broadcasted_iota(jnp.int32, (flat, top), 0), top)
    route_row = jnp.sum(jnp.where(j_row == at_row, by_row, 0.0), axis=0, keepdims=True)
    route_col = jnp.sum(jnp.where(j_col == at_col, by_col, 0.0), axis=1, keepdims=True)
    mine_ref[...] = route_row
    peers(lambda t: route_copy(t, me).start())
    keep_own(mine_ref, all_ref.at[me], r_recv)
    same = route_col == route_row
    rank_row = jnp.sum(jnp.where(same & (early < late), 1.0, 0.0), axis=0, keepdims=True)
    rank_col = jnp.sum(jnp.where(same & (late < early), 1.0, 0.0), axis=1, keepdims=True)

    def placed(route, rank, stride):
        kind = jnp.where(route >= n_ex, 1.0, 0.0)
        home = route - kind * n_ex
        away = jnp.where(home >= n_ex // 2, home - n_ex // 2, home + n_ex // 2)
        home = jnp.where(kind > 0.5, away, home)
        return (home * stride + kind * (slots // 2) + rank).astype(jnp.int32)

    pos_row = placed(route_row, rank_row, slots)
    pos_col = placed(route_col, rank_col, 2 * slots)

    wide = 2 * n_ex * slots
    lot = 8
    loads[2].wait()

    def pack(i, c):
        spot = lax.broadcasted_iota(jnp.int32, (lot * slots, flat), 0) + i * (lot * slots)
        hit = jnp.where(spot == pos_row, 1.0, 0.0).astype(BF16)
        v = jnp.dot(hit, cot_ref[...], preferred_element_type=F32).reshape(lot, slots, hidden)
        for j in range(lot):
            for k in range(6):
                dh_out[i * lot + j, k * slots:(k + 1) * slots, :] = v[
                    j, :, k * lane:(k + 1) * lane
                ].astype(BF16)
        return c

    lax.fori_loop(0, n_ex // lot, pack, 0)
    to_peers(lambda t: dh_copy(t, me, 0).start())
    keep_own(dh_piece(dh_out.at[me], 0), dh_piece(dh_in.at[me], 0), dh_recv.at[0])

    both_ways = [(h, sign) for h in range(2) for sign in (1, -1)]
    for h, sign in both_ways:
        arrived(h, -sign, 0)
        pass_on(h, -sign, 0, 0, sign, 0 if sign == 1 else 1)
    for h, sign in both_ways:
        pass_on(h, -sign, 0, 1, 1)
        pass_on(h, -sign, 0, 1, -1)
        share(h, -sign, 0)
    for h, sign in both_ways:
        arrived(h, 0, -sign)
        pass_on(h, 0, -sign, 1, sign, 0 if sign == 1 else 1)
        share(h, 0, -sign)
    for h in range(2):
        for piece in range(2):
            arrived(h, 2, 0, piece)
        for sign in (1, -1):
            pass_on(h, 2, 0, 1, sign)
        share(h, 2, 0)

    landed(all_ref, r_recv)
    for s in range(n_ex):
        flat_ref[s:s + 1, :] = all_ref[s]
    named = flat_ref[...]
    here = me.astype(F32)
    other = jnp.where(me >= n_ex // 2, me - n_ex // 2, me + n_ex // 2) + n_ex
    kinds = [jnp.where(named == v, 1.0, 0.0) for v in (here, other.astype(F32))]
    prior = jnp.where(early < late, 1.0, 0.0).astype(BF16)
    ranks = jnp.dot(
        jnp.concatenate(kinds, axis=0).astype(BF16), prior, preferred_element_type=F32
    )
    flat_ref[...] = (
        kinds[0] * (ranks[:n_ex] + 1.0) + kinds[1] * (ranks[n_ex:] + (1.0 + slots // 2)) - 1.0
    )
    token_lane = lax.broadcasted_iota(jnp.int32, (flat, 2 * tok), 1)
    token_lane = jnp.where(token_lane >= tok, token_lane - tok, token_lane) * top
    from_row = lax.broadcasted_iota(jnp.int32, (flat, 2 * tok), 0)
    to_token = jnp.where(
        (from_row >= token_lane) & (from_row < token_lane + top), 1.0, 0.0
    ).astype(BF16)
    spot_row = lax.broadcasted_iota(jnp.int32, (2 * slots, 2 * tok), 0) >= slots
    spot_lane = lax.broadcasted_iota(jnp.int32, (2 * slots, 2 * tok), 1) >= tok
    slot_no = lax.broadcasted_iota(jnp.int32, (slots, flat), 0).astype(F32)

    def choose(i, c):
        hits = [
            jnp.where(slot_no == flat_ref[pl.ds(2 * i + k, 1), :], 1.0, 0.0) for k in range(2)
        ]
        v = jnp.dot(
            jnp.concatenate(hits, axis=0).astype(BF16), to_token, preferred_element_type=F32
        )
        sel_ref[i] = jnp.where(spot_row == spot_lane, v, 0.0).astype(BF16)
        return c

    lax.fori_loop(0, n_ex // 2, choose, 0)

    for h in range(2):
        select(h, 0, 0)
    for h in range(2):
        for da in (1, -1):
            select(h, da, 0)
    for da in (1, -1, 2):
        for h, sign in both_ways:
            arrived(h, da, -sign)
            pass_on(h, da, -sign, 1, sign, 0 if sign == 1 else 1)
            share(h, da, -sign)
    to_peers(lambda t: dh_copy(t, me, 1).start())
    keep_own(dh_piece(dh_out.at[me], 1), dh_piece(dh_in.at[me], 1), dh_recv.at[1])
    for h in range(2):
        for da, db in ((0, 1), (0, -1), (2, 0), (1, 1), (1, -1), (-1, 1), (-1, -1)):
            select(h, da, db)
    for da in (0, 1, -1, 2):
        for h in range(2):
            for piece in range(2):
                arrived(h, da, 2, piece)
            share(h, da, 2)
    for h in range(2):
        for da, db in ((2, 1), (2, -1), (0, 2), (1, 2), (-1, 2), (2, 2)):
            select(h, da, db)
    for c in w_copies:
        c.wait()
    m_blk = rows // 2

    def gates(b):
        def one(i, c):
            r = pl.ds(pl.multiple_of(i * m_blk, m_blk), m_blk)
            for k in range(2):
                gate_ref[k, r] = jnp.dot(
                    xs_ref[r, :], w_ref[k, :, b * third:(b + 1) * third],
                    preferred_element_type=F32,
                )
            return c

        lax.fori_loop(0, 2, one, 0)

    def cotangents(b):
        def one(i, c):
            n = 2 * slots
            r = pl.ds(pl.multiple_of(i * n, n), n)
            v = dh_in[pl.ds(2 * i, 2), b * n:(b + 1) * n].astype(F32)
            for k in range(2):
                cs = slice(k * lane, (k + 1) * lane)
                h = v[:, k * slots:(k + 1) * slots].reshape(n, lane)
                g, u = gate_ref[0, r, cs], gate_ref[1, r, cs]
                s = jax.nn.sigmoid(g)
                at = b * third + k * lane
                d_ref[r, at:at + lane] = (h * u * s * (1.0 + g * (1.0 - s))).astype(BF16)
                d_ref[r, hidden + at:hidden + at + lane] = (h * g * s).astype(BF16)
            return c

        lax.fori_loop(0, n_ex // 2, one, 0)

    def part(c, k, b):
        x_cols = xs_ref[:, pl.ds(pl.multiple_of(c * cols, cols), cols)]
        at = k * hidden + b * third
        return lax.dot_general(
            x_cols, d_ref[:, at:at + third], over_first, preferred_element_type=F32
        )

    def chunk(s, k):
        return lax.rem(p + 2 * n_dp - 1 - s, n_dp) if k == 0 else lax.rem(p + 1 + s, n_dp)

    def ring_copy(s, k, b):
        return pltpu.make_async_remote_copy(
            src_ref=ring_ref.at[k, s, b],
            dst_ref=ring_ref.at[k, s + 1, b],
            send_sem=ring_send.at[k, s, b],
            recv_sem=ring_recv.at[k, s, b],
            device_id={"dp": right if k == 0 else left},
            device_id_type=MESH,
        )

    def begin(b):
        gates(b)
        if b < 2:
            landed(dh_piece(dh_in, b), dh_recv.at[b])
        cotangents(b)
        for k in range(2):
            ring_ref[k, 0, b] = part(chunk(0, k), k, b).astype(BF16)
            ring_copy(0, k, b).start()
        for k in range(2):
            part_ref[k, b] = part(chunk(1, k), k, b)

    def unit(s, b):
        for k in range(2):
            ring_copy(s - 1, k, b).wait_recv()
            ring_ref[k, s, b] = (ring_ref[k, s, b].astype(F32) + part_ref[k, b]).astype(BF16)
            ring_copy(s, k, b).start()
        for k in range(2):
            part_ref[k, b] = part(chunk(s + 1, k), k, b)

    begin(0)
    begin(1)
    unit(1, 0)
    begin(2)
    side = 8
    wide_col = width // 2

    def back_half(i, h):
        y = lax.rem(me // side + i, n_ex // side)
        r = pl.ds(pl.multiple_of(y * side * slots, side * slots), side * slots)
        wc = slice(h * wide_col, (h + 1) * wide_col)
        dims_back = (((1,), (1,)), ((), ()))
        b = lax.dot_general(
            d_ref[r, :hidden], w_ref[0, wc, :], dims_back, preferred_element_type=F32
        ) + lax.dot_general(
            d_ref[r, hidden:], w_ref[1, wc, :], dims_back, preferred_element_type=F32
        )
        part_rows = b.reshape(side, slots, wide_col)
        for j in range(side):
            back_ref[y * side + j, h * slots:(h + 1) * slots, :] = part_rows[j].astype(BF16)
        return y

    def ret_copy(t):
        return pltpu.make_async_remote_copy(
            src_ref=back_ref.at[t],
            dst_ref=ret_ref.at[me],
            send_sem=ret_send,
            recv_sem=ret_recv,
            device_id={"expert": t},
            device_id_type=MESH,
        )

    def start_returns(i, y):
        if i == 0:
            keep_own(back_ref.at[me], ret_ref.at[me], ret_recv)
        for dx in (1, 3, 0, 2):
            for dc in range(2):
                if (i, dx, dc) != (0, 0, 0):
                    ret_copy(y * side + lax.rem(mx + dx, SIDE) * 2 + lax.rem(core + dc, 2)).start()

    back_half(0, 0)
    unit(1, 1)
    start_returns(0, back_half(0, 1))
    unit(1, 2)
    back_half(1, 0)
    unit(2, 0)
    start_returns(1, back_half(1, 1))
    unit(2, 1)
    back_half(3, 0)
    unit(2, 2)
    start_returns(3, back_half(3, 1))
    unit(3, 0)
    back_half(2, 0)
    unit(3, 1)
    start_returns(2, back_half(2, 1))
    unit(3, 2)

    place = lax.broadcasted_iota(jnp.int32, (flat, wide), 1)
    for k in range(2):
        hit = jnp.where(place == pos_col + k * slots, 1.0, 0.0).astype(BF16)
        comb_ref[k * tok:(k + 1) * tok, :] = jnp.dot(
            group, hit, preferred_element_type=F32
        ).astype(BF16)

    def alone(s, c):
        for b in range(3):
            unit(s, b)
        return c

    lax.fori_loop(4, n_dp - 1, alone, 0)
    landed(ret_ref, ret_recv)
    summed = jnp.dot(
        comb_ref[...], ret_ref[...].reshape(wide, wide_col), preferred_element_type=F32
    )
    gt_buf[:, :wide_col] = summed[:tok].astype(BF16)
    gt_buf[:, wide_col:] = summed[tok:].astype(BF16)
    outs = [pltpu.make_async_copy(gt_buf, gt_ref, out_sem.at[6])]
    outs[0].start()

    scale = 1.0 / n_dp
    for b in range(3):
        for k, out in enumerate((gg_ref, gu_ref)):
            ring_copy(n_dp - 2, k, b).wait_recv()
            g_buf[k, b] = (ring_ref[k, n_dp - 1, b].astype(F32) + part_ref[k, b]) * scale
            outs.append(
                pltpu.make_async_copy(
                    g_buf.at[k, b], out.at[:, pl.ds(b * third, third)], out_sem.at[2 * b + k]
                )
            )
            outs[-1].start()

    def sent(s, c):
        for k in range(2):
            for b in range(3):
                ring_copy(s, k, b).wait_send()
        return c

    lax.fori_loop(0, n_dp - 1, sent, 0)
    for c in sends:
        c.wait_send()
    for c in outs:
        c.wait()
    others = pl.ds(0, n_ex - 1)
    landed(all_ref.at[others], r_send)
    landed(back_ref.at[others], ret_send)
    for q in range(2):
        landed(dh_piece(dh_out.at[others], q), dh_send.at[q])
    for h in range(2):
        for da in range(SIDE):
            for db in range(SIDE):
                sibling(h, da, db, core).wait_send()


def hand_over(a, b, c, x, y, z, u, v, w, sem):
    loads = [
        pltpu.make_async_copy(src, held, sem.at[0, k])
        for k, (src, held) in enumerate(((a, u), (b, v), (c, w)))
    ]
    stores = [
        pltpu.make_async_copy(held, dst, sem.at[1, k])
        for k, (held, dst) in enumerate(((u, x), (v, y), (w, z)))
    ]
    for copy in loads:
        copy.start()
    for load, store in zip(loads, stores):
        load.wait()
        store.start()
    for copy in stores:
        copy.wait()


def body(tokens, row_cotangent, routes, w_gate, w_up):
    n_ex, n_dp = lax.axis_size("expert"), lax.axis_size("dp")
    tok, width = tokens.shape
    top = routes.shape[1]
    hidden = w_gate.shape[2]
    capacity = 3 * tok * top // (4 * n_ex)
    slots = 2 * capacity
    rows = n_ex * slots
    flat = tok * top
    vmem = pl.BlockSpec(memory_space=pltpu.VMEM)
    hbm = pl.BlockSpec(memory_space=pl.ANY)
    cols = width // n_dp
    dma = pltpu.SemaphoreType.DMA
    grads = pl.pallas_call(
        functools.partial(expert_kernel, (n_dp, n_ex, slots, tok, top)),
        out_shape=(
            jax.ShapeDtypeStruct((tok, width), BF16),
            jax.ShapeDtypeStruct((cols, hidden), F32),
            jax.ShapeDtypeStruct((cols, hidden), F32),
        ),
        in_specs=[vmem, hbm, hbm, hbm, hbm],
        out_specs=(hbm, hbm, hbm),
        scratch_shapes=[
            pltpu.VMEM((2, width, hidden), BF16),
            pltpu.VMEM((rows, 2 * hidden), BF16),
            pltpu.VMEM((2, n_dp, 3, cols, hidden // 3), BF16),
            pltpu.VMEM((2, 3, cols, hidden // 3), F32),
            pltpu.VMEM((n_ex, 2 * slots, width // 2), BF16),
            pltpu.VMEM((n_ex, 2 * slots, width // 2), BF16),
            pltpu.VMEM((2 * tok, 2 * rows), BF16),
            pltpu.VMEM((flat, hidden), BF16),
            pltpu.VMEM((n_ex // 2, 2, 2 * tok, width // 2), BF16),
            pltpu.VMEM((rows, width), BF16),
            pltpu.VMEM((2, rows, hidden // 3), F32),
            pltpu.VMEM((n_ex, 6 * slots, hidden // 6), BF16),
            pltpu.VMEM((n_ex, 6 * slots, hidden // 6), BF16),
            pltpu.VMEM((n_ex, 1, flat), F32),
            pltpu.VMEM((n_ex, flat), F32),
            pltpu.VMEM((n_ex // 2, 2 * slots, 2 * tok), BF16),
            pltpu.VMEM((1, flat), F32),
            pltpu.VMEM((tok, width), BF16),
            pltpu.VMEM((2, 3, cols, hidden // 3), F32),
            dma((2,)),
            dma((2, n_dp, 3)),
            dma((2, n_dp, 3)),
            dma,
            dma,
            dma((7,)),
            dma((3,)),
            dma((40,)),
            dma((2, SIDE * SIDE, 2)),
            dma((2, SIDE * SIDE)),
            dma((2, SIDE * SIDE)),
            dma((2,)),
            dma((2,)),
            dma,
            dma,
        ],
        compiler_params=pltpu.CompilerParams(
            collective_id=0, has_side_effects=True, vmem_limit_bytes=56 << 20
        ),
        name="expert_backward",
    )(
        routes.T, tokens, row_cotangent.reshape(flat, hidden), w_gate[0], w_up[0],
    )
    gt, gg, gu = pl.pallas_call(
        hand_over,
        out_shape=tuple(jax.ShapeDtypeStruct(g.shape, g.dtype) for g in grads),
        in_specs=[hbm] * 3,
        out_specs=[hbm] * 3,
        scratch_shapes=[pltpu.VMEM(g.shape, g.dtype) for g in grads] + [dma((2, 3))],
        name="hand_over",
    )(*grads)
    return gt, gg[None], gu[None]


def solution(mesh):
    return jax.shard_map(
        body,
        mesh=mesh,
        in_specs=(
            P(("dp", "expert"), None),
            P(("dp", "expert"), None, None),
            P(("dp", "expert"), None),
            P("expert", None, None),
            P("expert", None, None),
        ),
        out_specs=(P(("dp", "expert"), None), P("expert", "dp", None), P("expert", "dp", None)),
        check_vma=False,
    )
```

```python
import functools

import jax
import jax.numpy as jnp
from jax import lax
from jax.experimental import pallas as pl
from jax.experimental.pallas import tpu as pltpu
from jax.sharding import PartitionSpec as P

MESH = pl.DeviceIdType.MESH
F32, BF16 = jnp.float32, jnp.bfloat16
SIDE = 4
ROUND = (
    (1, 0), (3, 0), (0, 1), (0, 3), (1, 1), (3, 3), (1, 3), (3, 1),
    (2, 0), (0, 2), (2, 1), (1, 2), (2, 3), (3, 2), (2, 2),
)


def expert_kernel(
    dims,
    routes_hbm, x_hbm, cot_hbm, wg_hbm, wu_hbm,
    gt_ref, gg_ref, gu_ref,
    w_ref, d_ref, ring_ref, part_ref, back_ref, ret_ref, comb_ref,
    cot_ref, xg_ref, xs_ref, gate_ref, dh_out, dh_in, all_ref, flat_ref, sel_ref,
    routes_ref, mine_ref, gt_buf, g_buf,
    w_sem, ring_send, ring_recv, ret_send, ret_recv, out_sem,
    in_sem, ag_send, ag_recv, sib_send, sib_recv, dh_send, dh_recv, r_send, r_recv,
):
    n_dp, n_ex, slots, tok, top = dims
    width, hidden = w_ref.shape[1], w_ref.shape[2]
    rows = n_ex * slots
    cols = width // n_dp
    third = hidden // 3
    lane = third // 2
    me = lax.axis_index("expert")
    p = lax.axis_index("dp")
    barrier = pltpu.get_barrier_semaphore()
    right, left = lax.rem(p + 1, n_dp), lax.rem(p + n_dp - 1, n_dp)
    for z in (left, right):
        pl.semaphore_signal(barrier, inc=1, device_id={"dp": z}, device_id_type=MESH)

    def greet(k, c):
        pl.semaphore_signal(
            barrier, inc=1, device_id={"expert": lax.rem(me + k, n_ex)}, device_id_type=MESH
        )
        return c

    lax.fori_loop(1, n_ex, greet, 0)

    core = lax.rem(me, 2)
    mx, my = lax.rem(me // 2, SIDE), me // (2 * SIDE)
    half_w = width // 2
    own_rows = pl.ds(pl.multiple_of(core * tok, tok), tok)
    loads = [
        pltpu.make_async_copy(
            x_hbm.at[:, pl.ds(h * half_w, half_w)], xg_ref.at[me // 2, h, own_rows], in_sem.at[h]
        )
        for h in range(2)
    ] + [
        pltpu.make_async_copy(cot_hbm, cot_ref, in_sem.at[2]),
        pltpu.make_async_copy(routes_hbm, routes_ref, in_sem.at[3]),
    ]
    w_copies = [
        pltpu.make_async_copy(src, w_ref.at[k], w_sem.at[k])
        for k, src in enumerate((wg_hbm, wu_hbm))
    ]
    for c in loads + w_copies:
        c.start()

    for c in loads[:2]:
        c.wait()

    def chip_at(h, da, db):
        dx, dy = (da, db) if h == 0 else (db, da)
        return lax.rem(my + dy, SIDE) * SIDE + lax.rem(mx + dx, SIDE)

    def off(da, db):
        return (da % SIDE) * SIDE + db % SIDE

    def slab(h, da, db, lo, n, of_core):
        return xg_ref.at[
            chip_at(h, da % SIDE, db % SIDE), h,
            pl.ds(pl.multiple_of(of_core * tok + lo, tok // 2), n),
        ]

    def pass_on(h, da, db, axis, sign, piece=None):
        lo, n = (0, tok) if piece is None else (piece * (tok // 2), tok // 2)
        ra, rb = (da - sign, db) if axis == 0 else (da, db - sign)
        ta, tb = (sign % SIDE, 0) if axis == 0 else (0, sign % SIDE)
        ref = slab(h, da, db, lo, n, core)
        c = pltpu.make_async_remote_copy(
            src_ref=ref, dst_ref=ref,
            send_sem=ag_send,
            recv_sem=ag_recv.at[h, off(ra, rb), piece or 0],
            device_id={"expert": chip_at(h, ta, tb) * 2 + core},
            device_id_type=MESH,
        )
        c.start()

    def arrived(h, da, db, piece=None):
        lo, n = (0, tok) if piece is None else (piece * (tok // 2), tok // 2)
        ref = slab(h, da, db, lo, n, core)
        pltpu.make_async_remote_copy(
            src_ref=ref, dst_ref=ref, send_sem=ag_send,
            recv_sem=ag_recv.at[h, off(da, db), piece or 0],
            device_id={"expert": me}, device_id_type=MESH,
        ).wait_recv()

    def sibling(h, da, db, of_core):
        ref = slab(h, da, db, 0, tok, of_core)
        return pltpu.make_async_remote_copy(
            src_ref=ref, dst_ref=ref,
            send_sem=sib_send,
            recv_sem=sib_recv.at[h, off(da, db)],
            device_id={"expert": me + 1 - 2 * core},
            device_id_type=MESH,
        )

    def share(h, da, db):
        sibling(h, da, db, core).start()

    def select(h, da, db):
        sibling(h, da, db, 1 - core).wait_recv()
        chip = chip_at(h, da % SIDE, db % SIDE)
        xs_ref[
            pl.ds(pl.multiple_of(chip * 2 * slots, 2 * slots), 2 * slots),
            h * half_w:(h + 1) * half_w,
        ] = jnp.dot(sel_ref[chip], xg_ref[chip, h], preferred_element_type=F32).astype(BF16)

    def route_copy(t, slot):
        return pltpu.make_async_remote_copy(
            src_ref=mine_ref, dst_ref=all_ref.at[slot],
            send_sem=r_send, recv_sem=r_recv,
            device_id={"expert": t}, device_id_type=MESH,
        )

    def dh_piece(ref, q):
        lanes = pl.ds(q * 2 * slots, 2 * (q + 1) * slots)
        return ref.at[:, lanes] if len(ref.shape) == 3 else ref.at[lanes]

    def dh_copy(t, slot, q):
        return pltpu.make_async_remote_copy(
            src_ref=dh_piece(dh_out.at[t], q), dst_ref=dh_piece(dh_in.at[slot], q),
            send_sem=dh_send.at[q], recv_sem=dh_recv.at[q],
            device_id={"expert": t}, device_id_type=MESH,
        )

    def landed(ref, sem):
        pltpu.make_async_copy(ref, ref, sem).wait()

    def keep_own(own, to, sem):
        pltpu.make_async_copy(own, to, sem).start()

    def peers(go):
        def one(k, c):
            go(lax.rem(me + k, n_ex))
            return c

        lax.fori_loop(1, n_ex, one, 0)

    def to_peers(go):
        for dx, dy in ROUND:
            for dc in range(2):
                go(chip_at(0, dx, dy) * 2 + lax.rem(core + dc, 2))
        go(me + 1 - 2 * core)

    pl.semaphore_wait(barrier, n_ex + 1)
    for h in range(2):
        for sign in (1, -1):
            pass_on(h, 0, 0, 0, sign)
    for h in range(2):
        for sign in (1, -1):
            pass_on(h, 0, 0, 1, sign)
        share(h, 0, 0)
    flat = tok * top
    early = lax.broadcasted_iota(jnp.int32, (flat, flat), 0)
    late = lax.broadcasted_iota(jnp.int32, (flat, flat), 1)
    row_of = lax.broadcasted_iota(jnp.int32, (tok, flat), 1)
    token_of = lax.broadcasted_iota(jnp.int32, (tok, flat), 0) * top
    group = jnp.where((row_of >= token_of) & (row_of < token_of + top), 1.0, 0.0).astype(BF16)
    loads[3].wait()
    named = routes_ref[...].astype(F32).astype(BF16)
    over_first = (((0,), (0,)), ((), ()))
    by_row = jnp.dot(named, group, preferred_element_type=F32)
    by_col = lax.dot_general(group, named, (((0,), (1,)), ((), ())), preferred_element_type=F32)
    j_row = lax.broadcasted_iota(jnp.int32, (top, flat), 0)
    j_col = lax.broadcasted_iota(jnp.int32, (flat, top), 1)
    at_row = lax.rem(lax.broadcasted_iota(jnp.int32, (top, flat), 1), top)
    at_col = lax.rem(lax.broadcasted_iota(jnp.int32, (flat, top), 0), top)
    route_row = jnp.sum(jnp.where(j_row == at_row, by_row, 0.0), axis=0, keepdims=True)
    route_col = jnp.sum(jnp.where(j_col == at_col, by_col, 0.0), axis=1, keepdims=True)
    mine_ref[...] = route_row
    peers(lambda t: route_copy(t, me).start())
    keep_own(mine_ref, all_ref.at[me], r_recv)
    same = route_col == route_row
    rank_row = jnp.sum(jnp.where(same & (early < late), 1.0, 0.0), axis=0, keepdims=True)
    rank_col = jnp.sum(jnp.where(same & (late < early), 1.0, 0.0), axis=1, keepdims=True)

    def placed(route, rank, stride):
        kind = jnp.where(route >= n_ex, 1.0, 0.0)
        home = route - kind * n_ex
        away = jnp.where(home >= n_ex // 2, home - n_ex // 2, home + n_ex // 2)
        home = jnp.where(kind > 0.5, away, home)
        return (home * stride + kind * (slots // 2) + rank).astype(jnp.int32)

    pos_row = placed(route_row, rank_row, slots)
    pos_col = placed(route_col, rank_col, 2 * slots)

    wide = 2 * n_ex * slots
    lot = 8
    loads[2].wait()

    def pack(i, c):
        spot = lax.broadcasted_iota(jnp.int32, (lot * slots, flat), 0) + i * (lot * slots)
        hit = jnp.where(spot == pos_row, 1.0, 0.0).astype(BF16)
        v = jnp.dot(hit, cot_ref[...], preferred_element_type=F32).reshape(lot, slots, hidden)
        for j in range(lot):
            for k in range(6):
                dh_out[i * lot + j, k * slots:(k + 1) * slots, :] = v[
                    j, :, k * lane:(k + 1) * lane
                ].astype(BF16)
        return c

    lax.fori_loop(0, n_ex // lot, pack, 0)
    to_peers(lambda t: dh_copy(t, me, 0).start())
    keep_own(dh_piece(dh_out.at[me], 0), dh_piece(dh_in.at[me], 0), dh_recv.at[0])

    both_ways = [(h, sign) for h in range(2) for sign in (1, -1)]
    for h, sign in both_ways:
        arrived(h, -sign, 0)
        pass_on(h, -sign, 0, 0, sign, 0 if sign == 1 else 1)
    for h, sign in both_ways:
        pass_on(h, -sign, 0, 1, 1)
        pass_on(h, -sign, 0, 1, -1)
        share(h, -sign, 0)
    for h, sign in both_ways:
        arrived(h, 0, -sign)
        pass_on(h, 0, -sign, 1, sign, 0 if sign == 1 else 1)
        share(h, 0, -sign)
    for h in range(2):
        for piece in range(2):
            arrived(h, 2, 0, piece)
        for sign in (1, -1):
            pass_on(h, 2, 0, 1, sign)
        share(h, 2, 0)

    landed(all_ref, r_recv)
    for s in range(n_ex):
        flat_ref[s:s + 1, :] = all_ref[s]
    named = flat_ref[...]
    here = me.astype(F32)
    other = jnp.where(me >= n_ex // 2, me - n_ex // 2, me + n_ex // 2) + n_ex
    kinds = [jnp.where(named == v, 1.0, 0.0) for v in (here, other.astype(F32))]
    prior = jnp.where(early < late, 1.0, 0.0).astype(BF16)
    ranks = jnp.dot(
        jnp.concatenate(kinds, axis=0).astype(BF16), prior, preferred_element_type=F32
    )
    flat_ref[...] = (
        kinds[0] * (ranks[:n_ex] + 1.0) + kinds[1] * (ranks[n_ex:] + (1.0 + slots // 2)) - 1.0
    )
    token_lane = lax.broadcasted_iota(jnp.int32, (flat, 2 * tok), 1)
    token_lane = jnp.where(token_lane >= tok, token_lane - tok, token_lane) * top
    from_row = lax.broadcasted_iota(jnp.int32, (flat, 2 * tok), 0)
    to_token = jnp.where(
        (from_row >= token_lane) & (from_row < token_lane + top), 1.0, 0.0
    ).astype(BF16)
    spot_row = lax.broadcasted_iota(jnp.int32, (2 * slots, 2 * tok), 0) >= slots
    spot_lane = lax.broadcasted_iota(jnp.int32, (2 * slots, 2 * tok), 1) >= tok
    slot_no = lax.broadcasted_iota(jnp.int32, (slots, flat), 0).astype(F32)

    def choose(i, c):
        hits = [
            jnp.where(slot_no == flat_ref[pl.ds(2 * i + k, 1), :], 1.0, 0.0) for k in range(2)
        ]
        v = jnp.dot(
            jnp.concatenate(hits, axis=0).astype(BF16), to_token, preferred_element_type=F32
        )
        sel_ref[i] = jnp.where(spot_row == spot_lane, v, 0.0).astype(BF16)
        return c

    lax.fori_loop(0, n_ex // 2, choose, 0)

    for h in range(2):
        select(h, 0, 0)
    for h in range(2):
        for da in (1, -1):
            select(h, da, 0)
    for da in (1, -1, 2):
        for h, sign in both_ways:
            arrived(h, da, -sign)
            pass_on(h, da, -sign, 1, sign, 0 if sign == 1 else 1)
            share(h, da, -sign)
    to_peers(lambda t: dh_copy(t, me, 1).start())
    keep_own(dh_piece(dh_out.at[me], 1), dh_piece(dh_in.at[me], 1), dh_recv.at[1])
    for h in range(2):
        for da, db in ((0, 1), (0, -1), (2, 0), (1, 1), (1, -1), (-1, 1), (-1, -1)):
            select(h, da, db)
    for c in w_copies:
        c.wait()
    m_blk = rows // 2

    def gate_block(b, at, n):
        r = pl.ds(pl.multiple_of(at, n), n)
        for k in range(2):
            gate_ref[k, r] = jnp.dot(
                xs_ref[r, :], w_ref[k, :, b * third:(b + 1) * third],
                preferred_element_type=F32,
            )

    def gates(b):
        def one(i, c):
            gate_block(b, i * m_blk, m_blk)
            return c

        lax.fori_loop(0, 2, one, 0)

    def cotangents(b):
        def one(i, c):
            n = 2 * slots
            r = pl.ds(pl.multiple_of(i * n, n), n)
            v = dh_in[pl.ds(2 * i, 2), b * n:(b + 1) * n].astype(F32)
            for k in range(2):
                cs = slice(k * lane, (k + 1) * lane)
                h = v[:, k * slots:(k + 1) * slots].reshape(n, lane)
                g, u = gate_ref[0, r, cs], gate_ref[1, r, cs]
                s = jax.nn.sigmoid(g)
                at = b * third + k * lane
                d_ref[r, at:at + lane] = (h * u * s * (1.0 + g * (1.0 - s))).astype(BF16)
                d_ref[r, hidden + at:hidden + at + lane] = (h * g * s).astype(BF16)
            return c

        lax.fori_loop(0, n_ex // 2, one, 0)

    def part(c, k, b):
        x_cols = xs_ref[:, pl.ds(pl.multiple_of(c * cols, cols), cols)]
        at = k * hidden + b * third
        return lax.dot_general(
            x_cols, d_ref[:, at:at + third], over_first, preferred_element_type=F32
        )

    def chunk(s, k):
        return lax.rem(p + 2 * n_dp - 1 - s, n_dp) if k == 0 else lax.rem(p + 1 + s, n_dp)

    def ring_copy(s, k, b):
        return pltpu.make_async_remote_copy(
            src_ref=ring_ref.at[k, s, b],
            dst_ref=ring_ref.at[k, s + 1, b],
            send_sem=ring_send,
            recv_sem=ring_recv.at[k, s, b],
            device_id={"dp": right if k == 0 else left},
            device_id_type=MESH,
        )

    def begin(b):
        if b:
            gates(b)
        if b < 2:
            landed(dh_piece(dh_in, b), dh_recv.at[b])
        cotangents(b)
        for k in range(2):
            ring_ref[k, 0, b] = part(chunk(0, k), k, b).astype(BF16)
            ring_copy(0, k, b).start()
        for k in range(2):
            part_ref[k, b] = part(chunk(1, k), k, b)

    def unit(s, b):
        for k in range(2):
            ring_copy(s - 1, k, b).wait_recv()
            ring_ref[k, s, b] = (ring_ref[k, s, b].astype(F32) + part_ref[k, b]).astype(BF16)
            ring_copy(s, k, b).start()
        for k in range(2):
            part_ref[k, b] = part(chunk(s + 1, k), k, b)

    y_blk = SIDE * 2 * slots

    def first_gates(dy):
        gate_block(0, lax.rem(my + dy, SIDE) * y_blk, y_blk)

    for da in (0, 1, -1):
        for h in range(2):
            for piece in range(2):
                arrived(h, da, 2, piece)
            share(h, da, 2)
    for h in range(2):
        for da, db in ((2, 1), (2, -1), (0, 2), (1, 2), (-1, 2)):
            select(h, da, db)
    first_gates(0)
    for h in range(2):
        for piece in range(2):
            arrived(h, 2, 2, piece)
        share(h, 2, 2)
    first_gates(1)
    first_gates(3)
    for h in range(2):
        select(h, 2, 2)
    first_gates(2)
    begin(0)
    begin(1)
    unit(1, 0)
    begin(2)
    side = 8
    wide_col = width // 2

    def back_half(i, h):
        y = lax.rem(me // side + i, n_ex // side)
        r = pl.ds(pl.multiple_of(y * side * slots, side * slots), side * slots)
        wc = slice(h * wide_col, (h + 1) * wide_col)
        dims_back = (((1,), (1,)), ((), ()))
        b = lax.dot_general(
            d_ref[r, :hidden], w_ref[0, wc, :], dims_back, preferred_element_type=F32
        ) + lax.dot_general(
            d_ref[r, hidden:], w_ref[1, wc, :], dims_back, preferred_element_type=F32
        )
        part_rows = b.reshape(side, slots, wide_col)
        for j in range(side):
            back_ref[y * side + j, h * slots:(h + 1) * slots, :] = part_rows[j].astype(BF16)
        return y

    def ret_copy(t):
        return pltpu.make_async_remote_copy(
            src_ref=back_ref.at[t],
            dst_ref=ret_ref.at[me],
            send_sem=ret_send,
            recv_sem=ret_recv,
            device_id={"expert": t},
            device_id_type=MESH,
        )

    def start_returns(i, y):
        if i == 0:
            keep_own(back_ref.at[me], ret_ref.at[me], ret_recv)
        for dx in (1, 3, 0, 2):
            for dc in range(2):
                if (i, dx, dc) != (0, 0, 0):
                    ret_copy(y * side + lax.rem(mx + dx, SIDE) * 2 + lax.rem(core + dc, 2)).start()

    back_half(0, 0)
    unit(1, 1)
    start_returns(0, back_half(0, 1))
    unit(1, 2)
    back_half(1, 0)
    unit(2, 0)
    start_returns(1, back_half(1, 1))
    unit(2, 1)
    back_half(3, 0)
    unit(2, 2)
    start_returns(3, back_half(3, 1))
    unit(3, 0)
    back_half(2, 0)
    unit(3, 1)
    start_returns(2, back_half(2, 1))
    unit(3, 2)

    place = lax.broadcasted_iota(jnp.int32, (flat, wide), 1)
    for k in range(2):
        hit = jnp.where(place == pos_col + k * slots, 1.0, 0.0).astype(BF16)
        comb_ref[k * tok:(k + 1) * tok, :] = jnp.dot(
            group, hit, preferred_element_type=F32
        ).astype(BF16)

    def alone(s, c):
        for b in range(3):
            unit(s, b)
        return c

    lax.fori_loop(4, n_dp - 1, alone, 0)
    landed(ret_ref, ret_recv)
    summed = jnp.dot(
        comb_ref[...], ret_ref[...].reshape(wide, wide_col), preferred_element_type=F32
    )
    gt_buf[:, :wide_col] = summed[:tok].astype(BF16)
    gt_buf[:, wide_col:] = summed[tok:].astype(BF16)
    outs = [pltpu.make_async_copy(gt_buf, gt_ref, out_sem.at[6])]
    outs[0].start()

    scale = 1.0 / n_dp
    for b in range(3):
        for k, out in enumerate((gg_ref, gu_ref)):
            ring_copy(n_dp - 2, k, b).wait_recv()
            g_buf[k, b] = (ring_ref[k, n_dp - 1, b].astype(F32) + part_ref[k, b]) * scale
            outs.append(
                pltpu.make_async_copy(
                    g_buf.at[k, b], out.at[:, pl.ds(b * third, third)], out_sem.at[2 * b + k]
                )
            )
            outs[-1].start()

    for c in outs:
        c.wait()
    landed(ring_ref.at[:, pl.ds(0, n_dp - 1)], ring_send)
    landed(xg_ref.at[pl.ds(0, n_ex // 2 - 1), 0], ag_send)
    landed(xg_ref.at[:, 0], sib_send)
    others = pl.ds(0, n_ex - 1)
    landed(all_ref.at[others], r_send)
    landed(back_ref.at[others], ret_send)
    for q in range(2):
        landed(dh_piece(dh_out.at[others], q), dh_send.at[q])


def hand_over(a, b, c, x, y, z, u, v, w, sem):
    loads = [
        pltpu.make_async_copy(src, held, sem.at[0, k])
        for k, (src, held) in enumerate(((a, u), (b, v), (c, w)))
    ]
    stores = [
        pltpu.make_async_copy(held, dst, sem.at[1, k])
        for k, (held, dst) in enumerate(((u, x), (v, y), (w, z)))
    ]
    for copy in loads:
        copy.start()
    for load, store in zip(loads, stores):
        load.wait()
        store.start()
    for copy in stores:
        copy.wait()


def body(tokens, row_cotangent, routes, w_gate, w_up):
    n_ex, n_dp = lax.axis_size("expert"), lax.axis_size("dp")
    tok, width = tokens.shape
    top = routes.shape[1]
    hidden = w_gate.shape[2]
    capacity = 3 * tok * top // (4 * n_ex)
    slots = 2 * capacity
    rows = n_ex * slots
    flat = tok * top
    vmem = pl.BlockSpec(memory_space=pltpu.VMEM)
    hbm = pl.BlockSpec(memory_space=pl.ANY)
    cols = width // n_dp
    dma = pltpu.SemaphoreType.DMA
    grads = pl.pallas_call(
        functools.partial(expert_kernel, (n_dp, n_ex, slots, tok, top)),
        out_shape=(
            jax.ShapeDtypeStruct((tok, width), BF16),
            jax.ShapeDtypeStruct((cols, hidden), F32),
            jax.ShapeDtypeStruct((cols, hidden), F32),
        ),
        in_specs=[hbm] * 5,
        out_specs=(hbm, hbm, hbm),
        scratch_shapes=[
            pltpu.VMEM((2, width, hidden), BF16),
            pltpu.VMEM((rows, 2 * hidden), BF16),
            pltpu.VMEM((2, n_dp, 3, cols, hidden // 3), BF16),
            pltpu.VMEM((2, 3, cols, hidden // 3), F32),
            pltpu.VMEM((n_ex, 2 * slots, width // 2), BF16),
            pltpu.VMEM((n_ex, 2 * slots, width // 2), BF16),
            pltpu.VMEM((2 * tok, 2 * rows), BF16),
            pltpu.VMEM((flat, hidden), BF16),
            pltpu.VMEM((n_ex // 2, 2, 2 * tok, width // 2), BF16),
            pltpu.VMEM((rows, width), BF16),
            pltpu.VMEM((2, rows, hidden // 3), F32),
            pltpu.VMEM((n_ex, 6 * slots, hidden // 6), BF16),
            pltpu.VMEM((n_ex, 6 * slots, hidden // 6), BF16),
            pltpu.VMEM((n_ex, 1, flat), F32),
            pltpu.VMEM((n_ex, flat), F32),
            pltpu.VMEM((n_ex // 2, 2 * slots, 2 * tok), BF16),
            pltpu.VMEM((top, tok), jnp.int32),
            pltpu.VMEM((1, flat), F32),
            pltpu.VMEM((tok, width), BF16),
            pltpu.VMEM((2, 3, cols, hidden // 3), F32),
            dma((2,)),
            dma,
            dma((2, n_dp, 3)),
            dma,
            dma,
            dma((7,)),
            dma((4,)),
            dma,
            dma((2, SIDE * SIDE, 2)),
            dma,
            dma((2, SIDE * SIDE)),
            dma((2,)),
            dma((2,)),
            dma,
            dma,
        ],
        compiler_params=pltpu.CompilerParams(
            collective_id=0, has_side_effects=True, vmem_limit_bytes=56 << 20
        ),
        name="expert_backward",
    )(
        routes.T, tokens, row_cotangent.reshape(flat, hidden), w_gate[0], w_up[0],
    )
    gt, gg, gu = pl.pallas_call(
        hand_over,
        out_shape=tuple(jax.ShapeDtypeStruct(g.shape, g.dtype) for g in grads),
        in_specs=[hbm] * 3,
        out_specs=[hbm] * 3,
        scratch_shapes=[pltpu.VMEM(g.shape, g.dtype) for g in grads] + [dma((2, 3))],
        name="hand_over",
    )(*grads)
    return gt, gg[None], gu[None]


def solution(mesh):
    return jax.shard_map(
        body,
        mesh=mesh,
        in_specs=(
            P(("dp", "expert"), None),
            P(("dp", "expert"), None, None),
            P(("dp", "expert"), None),
            P("expert", None, None),
            P("expert", None, None),
        ),
        out_specs=(P(("dp", "expert"), None), P("expert", "dp", None), P("expert", "dp", None)),
        check_vma=False,
    )
```

```python
import functools

import jax
import jax.numpy as jnp
from jax import lax
from jax.experimental import pallas as pl
from jax.experimental.pallas import tpu as pltpu
from jax.sharding import PartitionSpec as P

MESH = pl.DeviceIdType.MESH
F32, BF16 = jnp.float32, jnp.bfloat16
SIDE = 4
ROUND = (
    (1, 0), (3, 0), (0, 1), (0, 3), (1, 1), (3, 3), (1, 3), (3, 1),
    (2, 0), (0, 2), (2, 1), (1, 2), (2, 3), (3, 2), (2, 2),
)


def expert_kernel(
    dims,
    routes_hbm, x_hbm, cot_hbm, wg_hbm, wu_hbm,
    gt_ref, gg_ref, gu_ref,
    w_ref, d_ref, ring_ref, part_ref, back_ref, ret_ref, comb_ref,
    cot_ref, xg_ref, xs_ref, gate_ref, dh_out, dh_in, all_ref, flat_ref, sel_ref,
    routes_ref, mine_ref, gt_buf, g_buf,
    w_sem, ring_send, ring_recv, ret_send, ret_recv, out_sem,
    in_sem, ag_send, ag_recv, sib_send, sib_recv, dh_send, dh_recv, r_send, r_recv,
):
    n_dp, n_ex, slots, tok, top = dims
    width, hidden = w_ref.shape[1], w_ref.shape[2]
    rows = n_ex * slots
    cols = width // n_dp
    third = hidden // 3
    lane = third // 2
    me = lax.axis_index("expert")
    p = lax.axis_index("dp")
    barrier = pltpu.get_barrier_semaphore()
    right, left = lax.rem(p + 1, n_dp), lax.rem(p + n_dp - 1, n_dp)
    for z in (left, right):
        pl.semaphore_signal(barrier, inc=1, device_id={"dp": z}, device_id_type=MESH)

    def greet(k, c):
        pl.semaphore_signal(
            barrier, inc=1, device_id={"expert": lax.rem(me + k, n_ex)}, device_id_type=MESH
        )
        return c

    lax.fori_loop(1, n_ex, greet, 0)

    core = lax.rem(me, 2)
    mx, my = lax.rem(me // 2, SIDE), me // (2 * SIDE)
    half_w = width // 2
    own_rows = pl.ds(pl.multiple_of(core * tok, tok), tok)
    loads = [
        pltpu.make_async_copy(
            x_hbm.at[:, pl.ds(h * half_w, half_w)], xg_ref.at[me // 2, h, own_rows], in_sem.at[h]
        )
        for h in range(2)
    ] + [
        pltpu.make_async_copy(cot_hbm, cot_ref, in_sem.at[2]),
        pltpu.make_async_copy(routes_hbm, routes_ref, in_sem.at[3]),
    ]
    w_copies = [
        pltpu.make_async_copy(src, w_ref.at[k], w_sem.at[k])
        for k, src in enumerate((wg_hbm, wu_hbm))
    ]
    for c in loads + w_copies:
        c.start()

    for c in loads[:2]:
        c.wait()

    def chip_at(h, da, db):
        dx, dy = (da, db) if h == 0 else (db, da)
        return lax.rem(my + dy, SIDE) * SIDE + lax.rem(mx + dx, SIDE)

    def off(da, db):
        return (da % SIDE) * SIDE + db % SIDE

    def slab(h, da, db, lo, n, of_core):
        return xg_ref.at[
            chip_at(h, da % SIDE, db % SIDE), h,
            pl.ds(pl.multiple_of(of_core * tok + lo, tok // 2), n),
        ]

    def pass_on(h, da, db, axis, sign, piece=None):
        lo, n = (0, tok) if piece is None else (piece * (tok // 2), tok // 2)
        ra, rb = (da - sign, db) if axis == 0 else (da, db - sign)
        ta, tb = (sign % SIDE, 0) if axis == 0 else (0, sign % SIDE)
        ref = slab(h, da, db, lo, n, core)
        c = pltpu.make_async_remote_copy(
            src_ref=ref, dst_ref=ref,
            send_sem=ag_send,
            recv_sem=ag_recv.at[h, off(ra, rb), piece or 0],
            device_id={"expert": chip_at(h, ta, tb) * 2 + core},
            device_id_type=MESH,
        )
        c.start()

    def arrived(h, da, db, piece=None):
        lo, n = (0, tok) if piece is None else (piece * (tok // 2), tok // 2)
        ref = slab(h, da, db, lo, n, core)
        pltpu.make_async_remote_copy(
            src_ref=ref, dst_ref=ref, send_sem=ag_send,
            recv_sem=ag_recv.at[h, off(da, db), piece or 0],
            device_id={"expert": me}, device_id_type=MESH,
        ).wait_recv()

    def sibling(h, da, db, of_core):
        ref = slab(h, da, db, 0, tok, of_core)
        return pltpu.make_async_remote_copy(
            src_ref=ref, dst_ref=ref,
            send_sem=sib_send,
            recv_sem=sib_recv.at[h, off(da, db)],
            device_id={"expert": me + 1 - 2 * core},
            device_id_type=MESH,
        )

    def share(h, da, db):
        sibling(h, da, db, core).start()

    def select(h, da, db):
        sibling(h, da, db, 1 - core).wait_recv()
        chip = chip_at(h, da % SIDE, db % SIDE)
        xs_ref[
            pl.ds(pl.multiple_of(chip * 2 * slots, 2 * slots), 2 * slots),
            h * half_w:(h + 1) * half_w,
        ] = jnp.dot(sel_ref[chip], xg_ref[chip, h], preferred_element_type=F32).astype(BF16)

    def route_copy(t, slot):
        return pltpu.make_async_remote_copy(
            src_ref=mine_ref, dst_ref=all_ref.at[slot],
            send_sem=r_send, recv_sem=r_recv,
            device_id={"expert": t}, device_id_type=MESH,
        )

    def dh_piece(ref, q):
        lanes = pl.ds(q * 2 * slots, 2 * (q + 1) * slots)
        return ref.at[:, lanes] if len(ref.shape) == 3 else ref.at[lanes]

    def dh_copy(t, slot, q):
        return pltpu.make_async_remote_copy(
            src_ref=dh_piece(dh_out.at[t], q), dst_ref=dh_piece(dh_in.at[slot], q),
            send_sem=dh_send.at[q], recv_sem=dh_recv.at[q],
            device_id={"expert": t}, device_id_type=MESH,
        )

    def landed(ref, sem):
        pltpu.make_async_copy(ref, ref, sem).wait()

    def keep_own(own, to, sem):
        pltpu.make_async_copy(own, to, sem).start()

    def peers(go):
        def one(k, c):
            go(lax.rem(me + k, n_ex))
            return c

        lax.fori_loop(1, n_ex, one, 0)

    def to_peers(go):
        for dx, dy in ROUND:
            for dc in range(2):
                go(chip_at(0, dx, dy) * 2 + lax.rem(core + dc, 2))
        go(me + 1 - 2 * core)

    pl.semaphore_wait(barrier, n_ex + 1)
    for h in range(2):
        for sign in (1, -1):
            pass_on(h, 0, 0, 0, sign)
    for h in range(2):
        for sign in (1, -1):
            pass_on(h, 0, 0, 1, sign)
        share(h, 0, 0)
    flat = tok * top
    early = lax.broadcasted_iota(jnp.int32, (flat, flat), 0)
    late = lax.broadcasted_iota(jnp.int32, (flat, flat), 1)
    row_of = lax.broadcasted_iota(jnp.int32, (tok, flat), 1)
    token_of = lax.broadcasted_iota(jnp.int32, (tok, flat), 0) * top
    group = jnp.where((row_of >= token_of) & (row_of < token_of + top), 1.0, 0.0).astype(BF16)
    loads[3].wait()
    named = routes_ref[...].astype(F32).astype(BF16)
    over_first = (((0,), (0,)), ((), ()))
    by_row = jnp.dot(named, group, preferred_element_type=F32)
    by_col = lax.dot_general(group, named, (((0,), (1,)), ((), ())), preferred_element_type=F32)
    j_row = lax.broadcasted_iota(jnp.int32, (top, flat), 0)
    j_col = lax.broadcasted_iota(jnp.int32, (flat, top), 1)
    at_row = lax.rem(lax.broadcasted_iota(jnp.int32, (top, flat), 1), top)
    at_col = lax.rem(lax.broadcasted_iota(jnp.int32, (flat, top), 0), top)
    route_row = jnp.sum(jnp.where(j_row == at_row, by_row, 0.0), axis=0, keepdims=True)
    route_col = jnp.sum(jnp.where(j_col == at_col, by_col, 0.0), axis=1, keepdims=True)
    mine_ref[...] = route_row
    peers(lambda t: route_copy(t, me).start())
    keep_own(mine_ref, all_ref.at[me], r_recv)
    same = route_col == route_row
    rank_row = jnp.sum(jnp.where(same & (early < late), 1.0, 0.0), axis=0, keepdims=True)
    rank_col = jnp.sum(jnp.where(same & (late < early), 1.0, 0.0), axis=1, keepdims=True)

    def placed(route, rank, stride):
        kind = jnp.where(route >= n_ex, 1.0, 0.0)
        home = route - kind * n_ex
        away = jnp.where(home >= n_ex // 2, home - n_ex // 2, home + n_ex // 2)
        home = jnp.where(kind > 0.5, away, home)
        return (home * stride + kind * (slots // 2) + rank).astype(jnp.int32)

    pos_row = placed(route_row, rank_row, slots)
    pos_col = placed(route_col, rank_col, 2 * slots)

    wide = 2 * n_ex * slots
    lot = 8
    loads[2].wait()

    def pack(i, c):
        spot = lax.broadcasted_iota(jnp.int32, (lot * slots, flat), 0) + i * (lot * slots)
        hit = jnp.where(spot == pos_row, 1.0, 0.0).astype(BF16)
        v = jnp.dot(hit, cot_ref[...], preferred_element_type=F32).reshape(lot, slots, hidden)
        for j in range(lot):
            for b in range(3):
                both = [v[j, :, k * lane:(k + 1) * lane] for k in (2 * b, 2 * b + 1)]
                dh_out[i * lot + j, 2 * b * slots:2 * (b + 1) * slots, :] = jnp.concatenate(
                    both, axis=0
                ).astype(BF16)
        return c

    lax.fori_loop(0, n_ex // lot, pack, 0)
    to_peers(lambda t: dh_copy(t, me, 0).start())
    keep_own(dh_piece(dh_out.at[me], 0), dh_piece(dh_in.at[me], 0), dh_recv.at[0])

    both_ways = [(h, sign) for h in range(2) for sign in (1, -1)]
    for h, sign in both_ways:
        arrived(h, -sign, 0)
        pass_on(h, -sign, 0, 0, sign, 0 if sign == 1 else 1)
    for h, sign in both_ways:
        pass_on(h, -sign, 0, 1, 1)
        pass_on(h, -sign, 0, 1, -1)
        share(h, -sign, 0)
    for h, sign in both_ways:
        arrived(h, 0, -sign)
        pass_on(h, 0, -sign, 1, sign, 0 if sign == 1 else 1)
        share(h, 0, -sign)
    for h in range(2):
        for piece in range(2):
            arrived(h, 2, 0, piece)
        for sign in (1, -1):
            pass_on(h, 2, 0, 1, sign)
        share(h, 2, 0)

    landed(all_ref, r_recv)
    for s in range(n_ex):
        flat_ref[s:s + 1, :] = all_ref[s]
    named = flat_ref[...]
    here = me.astype(F32)
    other = jnp.where(me >= n_ex // 2, me - n_ex // 2, me + n_ex // 2) + n_ex
    kinds = [jnp.where(named == v, 1.0, 0.0) for v in (here, other.astype(F32))]
    prior = jnp.where(early < late, 1.0, 0.0).astype(BF16)
    ranks = jnp.dot(
        jnp.concatenate(kinds, axis=0).astype(BF16), prior, preferred_element_type=F32
    )
    flat_ref[...] = (
        kinds[0] * (ranks[:n_ex] + 1.0) + kinds[1] * (ranks[n_ex:] + (1.0 + slots // 2)) - 1.0
    )
    token_lane = lax.broadcasted_iota(jnp.int32, (flat, 2 * tok), 1)
    token_lane = jnp.where(token_lane >= tok, token_lane - tok, token_lane) * top
    from_row = lax.broadcasted_iota(jnp.int32, (flat, 2 * tok), 0)
    to_token = jnp.where(
        (from_row >= token_lane) & (from_row < token_lane + top), 1.0, 0.0
    ).astype(BF16)
    spot_row = lax.broadcasted_iota(jnp.int32, (2 * slots, 2 * tok), 0) >= slots
    spot_lane = lax.broadcasted_iota(jnp.int32, (2 * slots, 2 * tok), 1) >= tok
    slot_no = lax.broadcasted_iota(jnp.int32, (slots, flat), 0).astype(F32)

    def choose(i, c):
        hits = [
            jnp.where(slot_no == flat_ref[pl.ds(2 * i + k, 1), :], 1.0, 0.0) for k in range(2)
        ]
        v = jnp.dot(
            jnp.concatenate(hits, axis=0).astype(BF16), to_token, preferred_element_type=F32
        )
        sel_ref[i] = jnp.where(spot_row == spot_lane, v, 0.0).astype(BF16)
        return c

    lax.fori_loop(0, n_ex // 2, choose, 0)

    for h in range(2):
        select(h, 0, 0)
    for h in range(2):
        for da in (1, -1):
            select(h, da, 0)
    for da in (1, -1, 2):
        for h, sign in both_ways:
            arrived(h, da, -sign)
            pass_on(h, da, -sign, 1, sign, 0 if sign == 1 else 1)
            share(h, da, -sign)
    to_peers(lambda t: dh_copy(t, me, 1).start())
    keep_own(dh_piece(dh_out.at[me], 1), dh_piece(dh_in.at[me], 1), dh_recv.at[1])
    for h in range(2):
        for da, db in ((0, 1), (0, -1), (2, 0), (1, 1), (1, -1), (-1, 1), (-1, -1)):
            select(h, da, db)
    for c in w_copies:
        c.wait()
    m_blk = rows // 2

    def gate_block(b, at, n):
        r = pl.ds(pl.multiple_of(at, n), n)
        for k in range(2):
            gate_ref[k, r] = jnp.dot(
                xs_ref[r, :], w_ref[k, :, b * third:(b + 1) * third],
                preferred_element_type=F32,
            )

    def gates(b):
        def one(i, c):
            gate_block(b, i * m_blk, m_blk)
            return c

        lax.fori_loop(0, 2, one, 0)

    def cotangents(b):
        def one(i, c):
            n = 2 * slots
            r = pl.ds(pl.multiple_of(i * n, n), n)
            v = dh_in[pl.ds(2 * i, 2), b * n:(b + 1) * n].astype(F32)
            for k in range(2):
                cs = slice(k * lane, (k + 1) * lane)
                h = v[:, k * slots:(k + 1) * slots].reshape(n, lane)
                g, u = gate_ref[0, r, cs], gate_ref[1, r, cs]
                s = jax.nn.sigmoid(g)
                at = b * third + k * lane
                d_ref[r, at:at + lane] = (h * u * s * (1.0 + g * (1.0 - s))).astype(BF16)
                d_ref[r, hidden + at:hidden + at + lane] = (h * g * s).astype(BF16)
            return c

        lax.fori_loop(0, n_ex // 2, one, 0)

    def part(c, k, b):
        x_cols = xs_ref[:, pl.ds(pl.multiple_of(c * cols, cols), cols)]
        at = k * hidden + b * third
        return lax.dot_general(
            x_cols, d_ref[:, at:at + third], over_first, preferred_element_type=F32
        )

    def chunk(s, k):
        return lax.rem(p + 2 * n_dp - 1 - s, n_dp) if k == 0 else lax.rem(p + 1 + s, n_dp)

    def ring_copy(s, k, b):
        return pltpu.make_async_remote_copy(
            src_ref=ring_ref.at[k, s, b],
            dst_ref=ring_ref.at[k, s + 1, b],
            send_sem=ring_send,
            recv_sem=ring_recv.at[k, s, b],
            device_id={"dp": right if k == 0 else left},
            device_id_type=MESH,
        )

    def begin(b):
        if b == 2:
            gates(b)
        if b < 2:
            landed(dh_piece(dh_in, b), dh_recv.at[b])
        cotangents(b)
        for k in range(2):
            ring_ref[k, 0, b] = part(chunk(0, k), k, b).astype(BF16)
            ring_copy(0, k, b).start()
        for k in range(2):
            part_ref[k, b] = part(chunk(1, k), k, b)

    def unit(s, b):
        for k in range(2):
            ring_copy(s - 1, k, b).wait_recv()
            ring_ref[k, s, b] = (ring_ref[k, s, b].astype(F32) + part_ref[k, b]).astype(BF16)
            ring_copy(s, k, b).start()
        for k in range(2):
            part_ref[k, b] = part(chunk(s + 1, k), k, b)

    y_blk = SIDE * 2 * slots

    def first_gates(dy):
        gate_block(0, lax.rem(my + dy, SIDE) * y_blk, y_blk)

    for da in (0, 1, -1):
        for h in range(2):
            for piece in range(2):
                arrived(h, da, 2, piece)
            share(h, da, 2)
    for h in range(2):
        for da, db in ((2, 1), (2, -1), (0, 2), (1, 2), (-1, 2)):
            select(h, da, db)
    first_gates(0)
    for h in range(2):
        for piece in range(2):
            arrived(h, 2, 2, piece)
        share(h, 2, 2)
    first_gates(1)
    first_gates(3)
    for h in range(2):
        select(h, 2, 2)
    first_gates(2)
    begin(0)
    gates(1)
    unit(1, 0)
    begin(1)
    begin(2)
    unit(2, 0)
    side = 8
    wide_col = width // 2

    def back_half(i, h):
        y = lax.rem(me // side + i, n_ex // side)
        r = pl.ds(pl.multiple_of(y * side * slots, side * slots), side * slots)
        wc = slice(h * wide_col, (h + 1) * wide_col)
        dims_back = (((1,), (1,)), ((), ()))
        b = lax.dot_general(
            d_ref[r, :hidden], w_ref[0, wc, :], dims_back, preferred_element_type=F32
        ) + lax.dot_general(
            d_ref[r, hidden:], w_ref[1, wc, :], dims_back, preferred_element_type=F32
        )
        part_rows = b.reshape(side, slots, wide_col)
        for j in range(side):
            back_ref[y * side + j, h * slots:(h + 1) * slots, :] = part_rows[j].astype(BF16)
        return y

    def ret_copy(t):
        return pltpu.make_async_remote_copy(
            src_ref=back_ref.at[t],
            dst_ref=ret_ref.at[me],
            send_sem=ret_send,
            recv_sem=ret_recv,
            device_id={"expert": t},
            device_id_type=MESH,
        )

    def start_returns(i, y):
        if i == 0:
            keep_own(back_ref.at[me], ret_ref.at[me], ret_recv)
        for dx in (1, 3, 0, 2):
            for dc in range(2):
                if (i, dx, dc) != (0, 0, 0):
                    ret_copy(y * side + lax.rem(mx + dx, SIDE) * 2 + lax.rem(core + dc, 2)).start()

    back_half(0, 0)
    unit(1, 1)
    start_returns(0, back_half(0, 1))
    unit(1, 2)
    back_half(1, 0)
    start_returns(1, back_half(1, 1))
    unit(2, 1)
    back_half(3, 0)
    unit(2, 2)
    start_returns(3, back_half(3, 1))
    unit(3, 0)
    back_half(2, 0)
    unit(3, 1)
    start_returns(2, back_half(2, 1))
    unit(3, 2)

    place = lax.broadcasted_iota(jnp.int32, (flat, wide), 1)
    for k in range(2):
        hit = jnp.where(place == pos_col + k * slots, 1.0, 0.0).astype(BF16)
        comb_ref[k * tok:(k + 1) * tok, :] = jnp.dot(
            group, hit, preferred_element_type=F32
        ).astype(BF16)

    def alone(s, c):
        for b in range(3):
            unit(s, b)
        return c

    lax.fori_loop(4, n_dp - 1, alone, 0)
    landed(ret_ref, ret_recv)
    summed = jnp.dot(
        comb_ref[...], ret_ref[...].reshape(wide, wide_col), preferred_element_type=F32
    )
    gt_buf[:, :wide_col] = summed[:tok].astype(BF16)
    gt_buf[:, wide_col:] = summed[tok:].astype(BF16)
    outs = [pltpu.make_async_copy(gt_buf, gt_ref, out_sem.at[6])]
    outs[0].start()

    scale = 1.0 / n_dp
    for b in range(3):
        for k, out in enumerate((gg_ref, gu_ref)):
            ring_copy(n_dp - 2, k, b).wait_recv()
            g_buf[k, b] = (ring_ref[k, n_dp - 1, b].astype(F32) + part_ref[k, b]) * scale
            outs.append(
                pltpu.make_async_copy(
                    g_buf.at[k, b], out.at[:, pl.ds(b * third, third)], out_sem.at[2 * b + k]
                )
            )
            outs[-1].start()

    for c in outs:
        c.wait()
    landed(ring_ref.at[:, pl.ds(0, n_dp - 1)], ring_send)
    landed(xg_ref.at[pl.ds(0, n_ex // 2 - 1), 0], ag_send)
    landed(xg_ref.at[:, 0], sib_send)
    others = pl.ds(0, n_ex - 1)
    landed(all_ref.at[others], r_send)
    landed(back_ref.at[others], ret_send)
    for q in range(2):
        landed(dh_piece(dh_out.at[others], q), dh_send.at[q])


def hand_over(a, b, c, x, y, z, u, v, w, sem):
    loads = [
        pltpu.make_async_copy(src, held, sem.at[0, k])
        for k, (src, held) in enumerate(((a, u), (b, v), (c, w)))
    ]
    stores = [
        pltpu.make_async_copy(held, dst, sem.at[1, k])
        for k, (held, dst) in enumerate(((u, x), (v, y), (w, z)))
    ]
    for copy in loads:
        copy.start()
    for load, store in zip(loads, stores):
        load.wait()
        store.start()
    for copy in stores:
        copy.wait()


def body(tokens, row_cotangent, routes, w_gate, w_up):
    n_ex, n_dp = lax.axis_size("expert"), lax.axis_size("dp")
    tok, width = tokens.shape
    top = routes.shape[1]
    hidden = w_gate.shape[2]
    capacity = 3 * tok * top // (4 * n_ex)
    slots = 2 * capacity
    rows = n_ex * slots
    flat = tok * top
    vmem = pl.BlockSpec(memory_space=pltpu.VMEM)
    hbm = pl.BlockSpec(memory_space=pl.ANY)
    cols = width // n_dp
    dma = pltpu.SemaphoreType.DMA
    grads = pl.pallas_call(
        functools.partial(expert_kernel, (n_dp, n_ex, slots, tok, top)),
        out_shape=(
            jax.ShapeDtypeStruct((tok, width), BF16),
            jax.ShapeDtypeStruct((cols, hidden), F32),
            jax.ShapeDtypeStruct((cols, hidden), F32),
        ),
        in_specs=[hbm] * 5,
        out_specs=(hbm, hbm, hbm),
        scratch_shapes=[
            pltpu.VMEM((2, width, hidden), BF16),
            pltpu.VMEM((rows, 2 * hidden), BF16),
            pltpu.VMEM((2, n_dp, 3, cols, hidden // 3), BF16),
            pltpu.VMEM((2, 3, cols, hidden // 3), F32),
            pltpu.VMEM((n_ex, 2 * slots, width // 2), BF16),
            pltpu.VMEM((n_ex, 2 * slots, width // 2), BF16),
            pltpu.VMEM((2 * tok, 2 * rows), BF16),
            pltpu.VMEM((flat, hidden), BF16),
            pltpu.VMEM((n_ex // 2, 2, 2 * tok, width // 2), BF16),
            pltpu.VMEM((rows, width), BF16),
            pltpu.VMEM((2, rows, hidden // 3), F32),
            pltpu.VMEM((n_ex, 6 * slots, hidden // 6), BF16),
            pltpu.VMEM((n_ex, 6 * slots, hidden // 6), BF16),
            pltpu.VMEM((n_ex, 1, flat), F32),
            pltpu.VMEM((n_ex, flat), F32),
            pltpu.VMEM((n_ex // 2, 2 * slots, 2 * tok), BF16),
            pltpu.VMEM((top, tok), jnp.int32),
            pltpu.VMEM((1, flat), F32),
            pltpu.VMEM((tok, width), BF16),
            pltpu.VMEM((2, 3, cols, hidden // 3), F32),
            dma((2,)),
            dma,
            dma((2, n_dp, 3)),
            dma,
            dma,
            dma((7,)),
            dma((4,)),
            dma,
            dma((2, SIDE * SIDE, 2)),
            dma,
            dma((2, SIDE * SIDE)),
            dma((2,)),
            dma((2,)),
            dma,
            dma,
        ],
        compiler_params=pltpu.CompilerParams(
            collective_id=0, has_side_effects=True, vmem_limit_bytes=56 << 20
        ),
        name="expert_backward",
    )(
        routes.T, tokens, row_cotangent.reshape(flat, hidden), w_gate[0], w_up[0],
    )
    gt, gg, gu = pl.pallas_call(
        hand_over,
        out_shape=tuple(jax.ShapeDtypeStruct(g.shape, g.dtype) for g in grads),
        in_specs=[hbm] * 3,
        out_specs=[hbm] * 3,
        scratch_shapes=[pltpu.VMEM(g.shape, g.dtype) for g in grads] + [dma((2, 3))],
        name="hand_over",
    )(*grads)
    return gt, gg[None], gu[None]


def solution(mesh):
    return jax.shard_map(
        body,
        mesh=mesh,
        in_specs=(
            P(("dp", "expert"), None),
            P(("dp", "expert"), None, None),
            P(("dp", "expert"), None),
            P("expert", None, None),
            P("expert", None, None),
        ),
        out_specs=(P(("dp", "expert"), None), P("expert", "dp", None), P("expert", "dp", None)),
        check_vma=False,
    )
```

```python
import functools

import jax
import jax.numpy as jnp
from jax import lax
from jax.experimental import pallas as pl
from jax.experimental.pallas import tpu as pltpu
from jax.sharding import PartitionSpec as P

MESH = pl.DeviceIdType.MESH
F32, BF16 = jnp.float32, jnp.bfloat16
SIDE = 4
ROUND = (
    (1, 0), (3, 0), (0, 1), (0, 3), (1, 1), (3, 3), (1, 3), (3, 1),
    (2, 0), (0, 2), (2, 1), (1, 2), (2, 3), (3, 2), (2, 2),
)


def expert_kernel(
    dims,
    routes_hbm, x_hbm, cot_hbm, wg_hbm, wu_hbm,
    gt_ref, gg_ref, gu_ref,
    w_ref, d_ref, ring_ref, part_ref, back_ref, ret_ref, comb_ref,
    cot_ref, xg_ref, xs_ref, gate_ref, dh_out, dh_in, all_ref, flat_ref, sel_ref,
    routes_ref, mine_ref, gt_buf, g_buf,
    w_sem, ring_send, ring_recv, ret_send, ret_recv, out_sem,
    in_sem, ag_send, ag_recv, sib_send, sib_recv, dh_send, dh_recv, r_send, r_recv,
):
    n_dp, n_ex, slots, tok, top = dims
    width, hidden = w_ref.shape[1], w_ref.shape[2]
    rows = n_ex * slots
    cols = width // n_dp
    third = hidden // 3
    lane = third // 2
    me = lax.axis_index("expert")
    p = lax.axis_index("dp")
    barrier = pltpu.get_barrier_semaphore()
    right, left = lax.rem(p + 1, n_dp), lax.rem(p + n_dp - 1, n_dp)
    for z in (left, right):
        pl.semaphore_signal(barrier, inc=1, device_id={"dp": z}, device_id_type=MESH)

    def greet(k, c):
        pl.semaphore_signal(
            barrier, inc=1, device_id={"expert": lax.rem(me + k, n_ex)}, device_id_type=MESH
        )
        return c

    lax.fori_loop(1, n_ex, greet, 0)

    core = lax.rem(me, 2)
    mx, my = lax.rem(me // 2, SIDE), me // (2 * SIDE)
    half_w = width // 2
    own_rows = pl.ds(pl.multiple_of(core * tok, tok), tok)
    loads = [
        pltpu.make_async_copy(
            x_hbm.at[:, pl.ds(h * half_w, half_w)], xg_ref.at[me // 2, h, own_rows], in_sem.at[h]
        )
        for h in range(2)
    ] + [
        pltpu.make_async_copy(cot_hbm, cot_ref, in_sem.at[2]),
        pltpu.make_async_copy(routes_hbm, routes_ref, in_sem.at[3]),
    ]
    w_copies = [
        pltpu.make_async_copy(src, w_ref.at[k], w_sem.at[k])
        for k, src in enumerate((wg_hbm, wu_hbm))
    ]
    for c in loads + w_copies:
        c.start()

    for c in loads[:2]:
        c.wait()

    def chip_at(h, da, db):
        dx, dy = (da, db) if h == 0 else (db, da)
        return lax.rem(my + dy, SIDE) * SIDE + lax.rem(mx + dx, SIDE)

    def off(da, db):
        return (da % SIDE) * SIDE + db % SIDE

    def slab(h, da, db, lo, n, of_core):
        return xg_ref.at[
            chip_at(h, da % SIDE, db % SIDE), h,
            pl.ds(pl.multiple_of(of_core * tok + lo, tok // 2), n),
        ]

    def pass_on(h, da, db, axis, sign, piece=None):
        lo, n = (0, tok) if piece is None else (piece * (tok // 2), tok // 2)
        ra, rb = (da - sign, db) if axis == 0 else (da, db - sign)
        ta, tb = (sign % SIDE, 0) if axis == 0 else (0, sign % SIDE)
        ref = slab(h, da, db, lo, n, core)
        c = pltpu.make_async_remote_copy(
            src_ref=ref, dst_ref=ref,
            send_sem=ag_send,
            recv_sem=ag_recv.at[h, off(ra, rb), piece or 0],
            device_id={"expert": chip_at(h, ta, tb) * 2 + core},
            device_id_type=MESH,
        )
        c.start()

    def arrived(h, da, db, piece=None):
        lo, n = (0, tok) if piece is None else (piece * (tok // 2), tok // 2)
        ref = slab(h, da, db, lo, n, core)
        pltpu.make_async_remote_copy(
            src_ref=ref, dst_ref=ref, send_sem=ag_send,
            recv_sem=ag_recv.at[h, off(da, db), piece or 0],
            device_id={"expert": me}, device_id_type=MESH,
        ).wait_recv()

    def sibling(h, da, db, of_core):
        ref = slab(h, da, db, 0, tok, of_core)
        return pltpu.make_async_remote_copy(
            src_ref=ref, dst_ref=ref,
            send_sem=sib_send,
            recv_sem=sib_recv.at[h, off(da, db)],
            device_id={"expert": me + 1 - 2 * core},
            device_id_type=MESH,
        )

    def share(h, da, db):
        sibling(h, da, db, core).start()

    def select(h, da, db):
        sibling(h, da, db, 1 - core).wait_recv()
        chip = chip_at(h, da % SIDE, db % SIDE)
        xs_ref[
            pl.ds(pl.multiple_of(chip * 2 * slots, 2 * slots), 2 * slots),
            h * half_w:(h + 1) * half_w,
        ] = jnp.dot(sel_ref[chip], xg_ref[chip, h], preferred_element_type=F32).astype(BF16)

    def route_copy(t, slot):
        return pltpu.make_async_remote_copy(
            src_ref=mine_ref, dst_ref=all_ref.at[slot],
            send_sem=r_send, recv_sem=r_recv,
            device_id={"expert": t}, device_id_type=MESH,
        )

    def dh_piece(ref, q):
        lanes = pl.ds(q * 2 * slots, 2 * (q + 1) * slots)
        return ref.at[:, lanes] if len(ref.shape) == 3 else ref.at[lanes]

    def dh_copy(t, slot, q):
        return pltpu.make_async_remote_copy(
            src_ref=dh_piece(dh_out.at[t], q), dst_ref=dh_piece(dh_in.at[slot], q),
            send_sem=dh_send.at[q], recv_sem=dh_recv.at[q],
            device_id={"expert": t}, device_id_type=MESH,
        )

    def landed(ref, sem):
        pltpu.make_async_copy(ref, ref, sem).wait()

    def keep_own(own, to, sem):
        pltpu.make_async_copy(own, to, sem).start()

    def peers(go):
        def one(k, c):
            go(lax.rem(me + k, n_ex))
            return c

        lax.fori_loop(1, n_ex, one, 0)

    def to_peers(go):
        for dx, dy in ROUND:
            for dc in range(2):
                go(chip_at(0, dx, dy) * 2 + lax.rem(core + dc, 2))
        go(me + 1 - 2 * core)

    pl.semaphore_wait(barrier, n_ex + 1)
    for h in range(2):
        for sign in (1, -1):
            pass_on(h, 0, 0, 0, sign)
    for h in range(2):
        for sign in (1, -1):
            pass_on(h, 0, 0, 1, sign)
        share(h, 0, 0)
    flat = tok * top
    early = lax.broadcasted_iota(jnp.int32, (flat, flat), 0)
    late = lax.broadcasted_iota(jnp.int32, (flat, flat), 1)
    row_of = lax.broadcasted_iota(jnp.int32, (tok, flat), 1)
    token_of = lax.broadcasted_iota(jnp.int32, (tok, flat), 0) * top
    group = jnp.where((row_of >= token_of) & (row_of < token_of + top), 1.0, 0.0).astype(BF16)
    loads[3].wait()
    named = routes_ref[...].astype(F32).astype(BF16)
    over_first = (((0,), (0,)), ((), ()))
    by_row = jnp.dot(named, group, preferred_element_type=F32)
    by_col = lax.dot_general(group, named, (((0,), (1,)), ((), ())), preferred_element_type=F32)
    j_row = lax.broadcasted_iota(jnp.int32, (top, flat), 0)
    j_col = lax.broadcasted_iota(jnp.int32, (flat, top), 1)
    at_row = lax.rem(lax.broadcasted_iota(jnp.int32, (top, flat), 1), top)
    at_col = lax.rem(lax.broadcasted_iota(jnp.int32, (flat, top), 0), top)
    route_row = jnp.sum(jnp.where(j_row == at_row, by_row, 0.0), axis=0, keepdims=True)
    route_col = jnp.sum(jnp.where(j_col == at_col, by_col, 0.0), axis=1, keepdims=True)
    mine_ref[...] = route_row
    peers(lambda t: route_copy(t, me).start())
    keep_own(mine_ref, all_ref.at[me], r_recv)
    same = route_col == route_row
    rank_row = jnp.sum(jnp.where(same & (early < late), 1.0, 0.0), axis=0, keepdims=True)
    rank_col = jnp.sum(jnp.where(same & (late < early), 1.0, 0.0), axis=1, keepdims=True)

    def placed(route, rank, stride):
        kind = jnp.where(route >= n_ex, 1.0, 0.0)
        home = route - kind * n_ex
        away = jnp.where(home >= n_ex // 2, home - n_ex // 2, home + n_ex // 2)
        home = jnp.where(kind > 0.5, away, home)
        return (home * stride + kind * (slots // 2) + rank).astype(jnp.int32)

    pos_row = placed(route_row, rank_row, slots)
    pos_col = placed(route_col, rank_col, 2 * slots)

    wide = 2 * n_ex * slots
    lot = 8
    loads[2].wait()

    def pack(i, c):
        spot = lax.broadcasted_iota(jnp.int32, (lot * slots, flat), 0) + i * (lot * slots)
        hit = jnp.where(spot == pos_row, 1.0, 0.0).astype(BF16)
        v = jnp.dot(hit, cot_ref[...], preferred_element_type=F32).reshape(lot, slots, hidden)
        for j in range(lot):
            for b in range(3):
                both = [v[j, :, k * lane:(k + 1) * lane] for k in (2 * b, 2 * b + 1)]
                dh_out[i * lot + j, 2 * b * slots:2 * (b + 1) * slots, :] = jnp.concatenate(
                    both, axis=0
                ).astype(BF16)
        return c

    lax.fori_loop(0, n_ex // lot, pack, 0)

    both_ways = [(h, sign) for h in range(2) for sign in (1, -1)]
    for h, sign in both_ways:
        arrived(h, -sign, 0)
        pass_on(h, -sign, 0, 0, sign, 0 if sign == 1 else 1)
    for h, sign in both_ways:
        pass_on(h, -sign, 0, 1, 1)
        pass_on(h, -sign, 0, 1, -1)
        share(h, -sign, 0)
    for h, sign in both_ways:
        arrived(h, 0, -sign)
        pass_on(h, 0, -sign, 1, sign, 0 if sign == 1 else 1)
        share(h, 0, -sign)
    for h in range(2):
        for piece in range(2):
            arrived(h, 2, 0, piece)
        for sign in (1, -1):
            pass_on(h, 2, 0, 1, sign)
        share(h, 2, 0)

    to_peers(lambda t: dh_copy(t, me, 0).start())
    keep_own(dh_piece(dh_out.at[me], 0), dh_piece(dh_in.at[me], 0), dh_recv.at[0])

    landed(all_ref, r_recv)
    for s in range(n_ex):
        flat_ref[s:s + 1, :] = all_ref[s]
    named = flat_ref[...]
    here = me.astype(F32)
    other = jnp.where(me >= n_ex // 2, me - n_ex // 2, me + n_ex // 2) + n_ex
    kinds = [jnp.where(named == v, 1.0, 0.0) for v in (here, other.astype(F32))]
    prior = jnp.where(early < late, 1.0, 0.0).astype(BF16)
    ranks = jnp.dot(
        jnp.concatenate(kinds, axis=0).astype(BF16), prior, preferred_element_type=F32
    )
    flat_ref[...] = (
        kinds[0] * (ranks[:n_ex] + 1.0) + kinds[1] * (ranks[n_ex:] + (1.0 + slots // 2)) - 1.0
    )
    token_lane = lax.broadcasted_iota(jnp.int32, (flat, 2 * tok), 1)
    token_lane = jnp.where(token_lane >= tok, token_lane - tok, token_lane) * top
    from_row = lax.broadcasted_iota(jnp.int32, (flat, 2 * tok), 0)
    to_token = jnp.where(
        (from_row >= token_lane) & (from_row < token_lane + top), 1.0, 0.0
    ).astype(BF16)
    spot_row = lax.broadcasted_iota(jnp.int32, (2 * slots, 2 * tok), 0) >= slots
    spot_lane = lax.broadcasted_iota(jnp.int32, (2 * slots, 2 * tok), 1) >= tok
    slot_no = lax.broadcasted_iota(jnp.int32, (slots, flat), 0).astype(F32)

    def choose(i, c):
        hits = [
            jnp.where(slot_no == flat_ref[pl.ds(2 * i + k, 1), :], 1.0, 0.0) for k in range(2)
        ]
        v = jnp.dot(
            jnp.concatenate(hits, axis=0).astype(BF16), to_token, preferred_element_type=F32
        )
        sel_ref[i] = jnp.where(spot_row == spot_lane, v, 0.0).astype(BF16)
        return c

    lax.fori_loop(0, n_ex // 2, choose, 0)

    for h in range(2):
        select(h, 0, 0)
    for h in range(2):
        for da in (1, -1):
            select(h, da, 0)
    for da in (1, -1, 2):
        for h, sign in both_ways:
            arrived(h, da, -sign)
            pass_on(h, da, -sign, 1, sign, 0 if sign == 1 else 1)
            share(h, da, -sign)
    to_peers(lambda t: dh_copy(t, me, 1).start())
    keep_own(dh_piece(dh_out.at[me], 1), dh_piece(dh_in.at[me], 1), dh_recv.at[1])
    for h in range(2):
        for da, db in ((0, 1), (0, -1), (2, 0), (1, 1), (1, -1), (-1, 1), (-1, -1)):
            select(h, da, db)
    for c in w_copies:
        c.wait()
    m_blk = rows // 2

    def gate_block(b, at, n):
        r = pl.ds(pl.multiple_of(at, n), n)
        for k in range(2):
            gate_ref[k, r] = jnp.dot(
                xs_ref[r, :], w_ref[k, :, b * third:(b + 1) * third],
                preferred_element_type=F32,
            )

    def gates(b):
        def one(i, c):
            gate_block(b, i * m_blk, m_blk)
            return c

        lax.fori_loop(0, 2, one, 0)

    def cotangents(b):
        def one(i, c):
            n = 2 * slots
            r = pl.ds(pl.multiple_of(i * n, n), n)
            v = dh_in[pl.ds(2 * i, 2), b * n:(b + 1) * n].astype(F32)
            for k in range(2):
                cs = slice(k * lane, (k + 1) * lane)
                h = v[:, k * slots:(k + 1) * slots].reshape(n, lane)
                g, u = gate_ref[0, r, cs], gate_ref[1, r, cs]
                s = jax.nn.sigmoid(g)
                at = b * third + k * lane
                d_ref[r, at:at + lane] = (h * u * s * (1.0 + g * (1.0 - s))).astype(BF16)
                d_ref[r, hidden + at:hidden + at + lane] = (h * g * s).astype(BF16)
            return c

        lax.fori_loop(0, n_ex // 2, one, 0)

    def part(c, k, b):
        x_cols = xs_ref[:, pl.ds(pl.multiple_of(c * cols, cols), cols)]
        at = k * hidden + b * third
        return lax.dot_general(
            x_cols, d_ref[:, at:at + third], over_first, preferred_element_type=F32
        )

    def chunk(s, k):
        return lax.rem(p + 2 * n_dp - 1 - s, n_dp) if k == 0 else lax.rem(p + 1 + s, n_dp)

    def ring_copy(s, k, b):
        return pltpu.make_async_remote_copy(
            src_ref=ring_ref.at[k, s, b],
            dst_ref=ring_ref.at[k, s + 1, b],
            send_sem=ring_send,
            recv_sem=ring_recv.at[k, s, b],
            device_id={"dp": right if k == 0 else left},
            device_id_type=MESH,
        )

    def begin(b):
        if b == 2:
            gates(b)
        if b < 2:
            landed(dh_piece(dh_in, b), dh_recv.at[b])
        cotangents(b)
        for k in range(2):
            ring_ref[k, 0, b] = part(chunk(0, k), k, b).astype(BF16)
            ring_copy(0, k, b).start()
        for k in range(2):
            part_ref[k, b] = part(chunk(1, k), k, b)

    def unit(s, b):
        for k in range(2):
            ring_copy(s - 1, k, b).wait_recv()
            ring_ref[k, s, b] = (ring_ref[k, s, b].astype(F32) + part_ref[k, b]).astype(BF16)
            ring_copy(s, k, b).start()
        for k in range(2):
            part_ref[k, b] = part(chunk(s + 1, k), k, b)

    y_blk = SIDE * 2 * slots

    def first_gates(dy):
        gate_block(0, lax.rem(my + dy, SIDE) * y_blk, y_blk)

    for da in (0, 1, -1):
        for h in range(2):
            for piece in range(2):
                arrived(h, da, 2, piece)
            share(h, da, 2)
    for h in range(2):
        for da, db in ((2, 1), (2, -1), (0, 2), (1, 2), (-1, 2)):
            select(h, da, db)
    first_gates(0)
    for h in range(2):
        for piece in range(2):
            arrived(h, 2, 2, piece)
        share(h, 2, 2)
    first_gates(1)
    first_gates(3)
    for h in range(2):
        select(h, 2, 2)
    first_gates(2)
    begin(0)
    gates(1)
    unit(1, 0)
    begin(1)
    begin(2)
    unit(2, 0)
    side = 8
    wide_col = width // 2

    def back_half(i, h):
        y = lax.rem(me // side + i, n_ex // side)
        r = pl.ds(pl.multiple_of(y * side * slots, side * slots), side * slots)
        wc = slice(h * wide_col, (h + 1) * wide_col)
        dims_back = (((1,), (1,)), ((), ()))
        b = lax.dot_general(
            d_ref[r, :hidden], w_ref[0, wc, :], dims_back, preferred_element_type=F32
        ) + lax.dot_general(
            d_ref[r, hidden:], w_ref[1, wc, :], dims_back, preferred_element_type=F32
        )
        part_rows = b.reshape(side, slots, wide_col)
        for j in range(side):
            back_ref[y * side + j, h * slots:(h + 1) * slots, :] = part_rows[j].astype(BF16)
        return y

    def ret_copy(t):
        return pltpu.make_async_remote_copy(
            src_ref=back_ref.at[t],
            dst_ref=ret_ref.at[me],
            send_sem=ret_send,
            recv_sem=ret_recv,
            device_id={"expert": t},
            device_id_type=MESH,
        )

    def start_returns(i, y):
        if i == 0:
            keep_own(back_ref.at[me], ret_ref.at[me], ret_recv)
        for dx in (1, 3, 0, 2):
            for dc in range(2):
                if (i, dx, dc) != (0, 0, 0):
                    ret_copy(y * side + lax.rem(mx + dx, SIDE) * 2 + lax.rem(core + dc, 2)).start()

    back_half(0, 0)
    unit(1, 1)
    start_returns(0, back_half(0, 1))
    unit(1, 2)
    back_half(1, 0)
    start_returns(1, back_half(1, 1))
    unit(2, 1)
    back_half(3, 0)
    unit(2, 2)
    start_returns(3, back_half(3, 1))
    unit(3, 0)
    back_half(2, 0)
    unit(3, 1)
    start_returns(2, back_half(2, 1))
    unit(3, 2)

    place = lax.broadcasted_iota(jnp.int32, (flat, wide), 1)
    for k in range(2):
        hit = jnp.where(place == pos_col + k * slots, 1.0, 0.0).astype(BF16)
        comb_ref[k * tok:(k + 1) * tok, :] = jnp.dot(
            group, hit, preferred_element_type=F32
        ).astype(BF16)

    def alone(s, c):
        for b in range(3):
            unit(s, b)
        return c

    lax.fori_loop(4, n_dp - 1, alone, 0)
    landed(ret_ref, ret_recv)
    summed = jnp.dot(
        comb_ref[...], ret_ref[...].reshape(wide, wide_col), preferred_element_type=F32
    )
    gt_buf[:, :wide_col] = summed[:tok].astype(BF16)
    gt_buf[:, wide_col:] = summed[tok:].astype(BF16)
    outs = [pltpu.make_async_copy(gt_buf, gt_ref, out_sem.at[6])]
    outs[0].start()

    scale = 1.0 / n_dp
    for b in range(3):
        for k, out in enumerate((gg_ref, gu_ref)):
            ring_copy(n_dp - 2, k, b).wait_recv()
            g_buf[k, b] = (ring_ref[k, n_dp - 1, b].astype(F32) + part_ref[k, b]) * scale
            outs.append(
                pltpu.make_async_copy(
                    g_buf.at[k, b], out.at[:, pl.ds(b * third, third)], out_sem.at[2 * b + k]
                )
            )
            outs[-1].start()

    for c in outs:
        c.wait()
    landed(ring_ref.at[:, pl.ds(0, n_dp - 1)], ring_send)
    landed(xg_ref.at[pl.ds(0, n_ex // 2 - 1), 0], ag_send)
    landed(xg_ref.at[:, 0], sib_send)
    others = pl.ds(0, n_ex - 1)
    landed(all_ref.at[others], r_send)
    landed(back_ref.at[others], ret_send)
    for q in range(2):
        landed(dh_piece(dh_out.at[others], q), dh_send.at[q])


def hand_over(a, b, c, x, y, z, u, v, w, sem):
    loads = [
        pltpu.make_async_copy(src, held, sem.at[0, k])
        for k, (src, held) in enumerate(((a, u), (b, v), (c, w)))
    ]
    stores = [
        pltpu.make_async_copy(held, dst, sem.at[1, k])
        for k, (held, dst) in enumerate(((u, x), (v, y), (w, z)))
    ]
    for copy in loads:
        copy.start()
    for load, store in zip(loads, stores):
        load.wait()
        store.start()
    for copy in stores:
        copy.wait()


def body(tokens, row_cotangent, routes, w_gate, w_up):
    n_ex, n_dp = lax.axis_size("expert"), lax.axis_size("dp")
    tok, width = tokens.shape
    top = routes.shape[1]
    hidden = w_gate.shape[2]
    capacity = 3 * tok * top // (4 * n_ex)
    slots = 2 * capacity
    rows = n_ex * slots
    flat = tok * top
    vmem = pl.BlockSpec(memory_space=pltpu.VMEM)
    hbm = pl.BlockSpec(memory_space=pl.ANY)
    cols = width // n_dp
    dma = pltpu.SemaphoreType.DMA
    grads = pl.pallas_call(
        functools.partial(expert_kernel, (n_dp, n_ex, slots, tok, top)),
        out_shape=(
            jax.ShapeDtypeStruct((tok, width), BF16),
            jax.ShapeDtypeStruct((cols, hidden), F32),
            jax.ShapeDtypeStruct((cols, hidden), F32),
        ),
        in_specs=[hbm] * 5,
        out_specs=(hbm, hbm, hbm),
        scratch_shapes=[
            pltpu.VMEM((2, width, hidden), BF16),
            pltpu.VMEM((rows, 2 * hidden), BF16),
            pltpu.VMEM((2, n_dp, 3, cols, hidden // 3), BF16),
            pltpu.VMEM((2, 3, cols, hidden // 3), F32),
            pltpu.VMEM((n_ex, 2 * slots, width // 2), BF16),
            pltpu.VMEM((n_ex, 2 * slots, width // 2), BF16),
            pltpu.VMEM((2 * tok, 2 * rows), BF16),
            pltpu.VMEM((flat, hidden), BF16),
            pltpu.VMEM((n_ex // 2, 2, 2 * tok, width // 2), BF16),
            pltpu.VMEM((rows, width), BF16),
            pltpu.VMEM((2, rows, hidden // 3), F32),
            pltpu.VMEM((n_ex, 6 * slots, hidden // 6), BF16),
            pltpu.VMEM((n_ex, 6 * slots, hidden // 6), BF16),
            pltpu.VMEM((n_ex, 1, flat), F32),
            pltpu.VMEM((n_ex, flat), F32),
            pltpu.VMEM((n_ex // 2, 2 * slots, 2 * tok), BF16),
            pltpu.VMEM((top, tok), jnp.int32),
            pltpu.VMEM((1, flat), F32),
            pltpu.VMEM((tok, width), BF16),
            pltpu.VMEM((2, 3, cols, hidden // 3), F32),
            dma((2,)),
            dma,
            dma((2, n_dp, 3)),
            dma,
            dma,
            dma((7,)),
            dma((4,)),
            dma,
            dma((2, SIDE * SIDE, 2)),
            dma,
            dma((2, SIDE * SIDE)),
            dma((2,)),
            dma((2,)),
            dma,
            dma,
        ],
        compiler_params=pltpu.CompilerParams(
            collective_id=0, has_side_effects=True, vmem_limit_bytes=56 << 20
        ),
        name="expert_backward",
    )(
        routes.T, tokens, row_cotangent.reshape(flat, hidden), w_gate[0], w_up[0],
    )
    gt, gg, gu = pl.pallas_call(
        hand_over,
        out_shape=tuple(jax.ShapeDtypeStruct(g.shape, g.dtype) for g in grads),
        in_specs=[hbm] * 3,
        out_specs=[hbm] * 3,
        scratch_shapes=[pltpu.VMEM(g.shape, g.dtype) for g in grads] + [dma((2, 3))],
        name="hand_over",
    )(*grads)
    return gt, gg[None], gu[None]


def solution(mesh):
    return jax.shard_map(
        body,
        mesh=mesh,
        in_specs=(
            P(("dp", "expert"), None),
            P(("dp", "expert"), None, None),
            P(("dp", "expert"), None),
            P("expert", None, None),
            P("expert", None, None),
        ),
        out_specs=(P(("dp", "expert"), None), P("expert", "dp", None), P("expert", "dp", None)),
        check_vma=False,
    )
```
